512 devices in a mesh: section: 16 (over y, x), tp: 32 (over z, core).
Axes of the slice: x: 4, y: 4, z: 16, core: 2. Of those that a mesh axis runs over, the one named last changes fastest.
Arguments:
- hidden: bfloat16 [16, 128, 8192], P('section', 'tp'), may hold values from -6 to 6
- norm_gain: float32 [16, 8192], P('section'), may hold values from 0.25 to 1.75
- q_gain: float32 [16, 8192], P('section'), may hold values from 0.1 to 40, as said below
- out_weight: bfloat16 [16, 8192, 8192], P('section', 'tp'), may hold values from -0.0625 to 0.0625
- positions: int32 [16, 128], P('section'), may hold values from 0 to 127, as said below
Outputs:
- advanced: bfloat16 [16, 128, 8192], P('section', 'tp')
The draws below stay inside these ranges and needn't reach their ends.
Inputs may be any that keep to these rules, and one draw needn't show every extreme that they name: `q_gain`: positive gains; in each layer some heads' gains may be several times larger than the others'. `positions`: each micro-batch is a run of whole documents: position 0 starts a document and each next token's position is one more; one micro-batch of every draw is a single document.
All inputs are finite; a program needn't handle non-finite values. Where the reference program divides by a largest or mean magnitude, that divisor is 1e-20 or more.
Results may differ from the reference program's by a relative error of at most 0.03.
Values may be sent and summed in bfloat16 or wider, within the bound.
A program may use at most 64 MiB of HBM per device.

```python
import math
import jax
import jax.numpy as jnp
from jax import lax

D = 8192
HEAD = 128
BLOCK = 128
TOK_MB = 128
TICKS = 2
HEADS = 64
GROUPS = 32
N_SECTION = 16


def draw_q_gain(key, part):
    key = jax.random.fold_in(key, 7)
    base_key = jax.random.fold_in(key, 0)
    logs = jax.random.uniform(base_key, (N_SECTION, D), jnp.float32, math.log(0.1), math.log(1.0))
    gains = jnp.exp(logs)
    return gains


def draw_positions(key, part):
    key = jax.random.fold_in(key, 5)
    cut_key, row_key = jax.random.split(key)
    cuts = jax.random.randint(cut_key, (N_SECTION, TOK_MB), 0, 32) == 0
    index = lax.broadcasted_iota(jnp.int32, (N_SECTION, TOK_MB), 1)
    section_ids = lax.broadcasted_iota(jnp.int32, (N_SECTION, TOK_MB), 0)
    single = jax.random.randint(row_key, (), 0, N_SECTION)
    cuts = jnp.where(section_ids == single, False, cuts)
    cuts = jnp.where(index == 0, True, cuts)
    starts = jnp.where(cuts, index, 0)
    last = lax.cummax(starts, axis=1)
    return (index - last).astype(jnp.int32)


def level_of(own_key, dims, cuts, least, high):
    def one(position, shards_of):
        draws = jax.random.uniform(jax.random.fold_in(jax.random.fold_in(own_key, 6), position), (shards_of,), jnp.float32, least / len(cuts), high / len(cuts))
        return jnp.repeat(jnp.exp(draws), dims[position] // shards_of).reshape((-1,) + (1,) * (len(dims) - position - 1))

    loudness = one(*cuts[0])
    for cut in cuts[1:]:
        loudness = loudness * one(*cut)
    return loudness


def centred(own_key, shape, scale, reach, cuts=(), kind=jnp.bfloat16):
    array = jax.random.normal(own_key, shape, jnp.float32) * scale
    if len(cuts) > 0:
        array = level_of(own_key, shape, cuts, -0.22, 0.18) * array
    return jnp.clip(array, min=-reach, max=reach).astype(kind)


def setup_inputs(seed: int = 0) -> dict:
    seeds = jax.random.split(jax.random.key(seed), 6)
    hidden = centred(seeds[0], (N_SECTION, TOK_MB, D), 1.0, 6.0, ((0, 16), (1, 32)))
    norm_gain = jnp.clip(1.0 + 0.15 * jax.random.normal(seeds[1], (N_SECTION, D), jnp.float32), 0.25, 1.75)
    q_gain = draw_q_gain(jax.random.fold_in(seeds[5], 71), 0)
    out_weight = centred(seeds[3], (N_SECTION, D, D), D ** -0.5, 0.0625, ((0, 16), (1, 32)))
    positions = draw_positions(jax.random.fold_in(seeds[5], 71), 0)
    return dict(hidden=hidden, norm_gain=norm_gain, q_gain=q_gain, out_weight=out_weight, positions=positions)


code_limit = 3.0

def sign_table(width):
    rows = lax.broadcasted_iota(jnp.int32, (width, width), 0)
    cols = lax.broadcasted_iota(jnp.int32, (width, width), 1)
    both = jnp.bitwise_and(rows, cols)
    parity = jnp.zeros((width, width), jnp.int32)
    for place in range(width.bit_length() - 1):
        parity = parity + jnp.bitwise_and(jnp.right_shift(both, place), 1)
    return (1 - 2 * jnp.bitwise_and(parity, 1)).astype(jnp.float32)

def section_layer(table, operands):
    state, gain, qgain, weight, pos = operands
    tokens = state.shape[0]
    width = state.shape[1]
    blocks = width // BLOCK
    flat = state.astype(jnp.float32)
    meansq = lax.optimization_barrier(jnp.mean(flat * flat, axis=-1, keepdims=True))
    normed = (flat * lax.rsqrt(meansq + 1e-05) * gain).astype(jnp.bfloat16)
    keys = normed.reshape(tokens, HEADS, HEAD)
    query = (keys.astype(jnp.float32) * qgain.reshape(HEADS, HEAD)).astype(jnp.bfloat16)
    scores = jnp.einsum('thd,shd->hts', query.astype(jnp.float32), keys.astype(jnp.float32)) * HEAD ** (-0.5)
    row_ids = lax.broadcasted_iota(jnp.int32, (tokens, tokens), 0)
    col_ids = lax.broadcasted_iota(jnp.int32, (tokens, tokens), 1)
    seen = (col_ids <= row_ids) & (col_ids >= row_ids - pos[:, None])
    scores = jnp.where(seen[None], scores, -1e+30)
    top = lax.optimization_barrier(jnp.max(scores, axis=-1, keepdims=True))
    expo = jnp.where(seen[None], jnp.exp(scores - top), 0.0)
    weights = (expo / lax.optimization_barrier(jnp.sum(expo, axis=-1, keepdims=True))).astype(jnp.bfloat16)
    context = jnp.einsum('hts,shd->thd', weights.astype(jnp.float32), keys.astype(jnp.float32))
    context = context.astype(jnp.bfloat16).reshape(tokens, width)
    grouped = context.reshape(tokens, GROUPS, width // GROUPS).astype(jnp.float32)
    split_weight = weight.reshape(GROUPS, width // GROUPS, width).astype(jnp.float32)
    partial_value = jnp.einsum('tgk,gkd->gtd', grouped, split_weight).astype(jnp.bfloat16)
    pieces = partial_value.astype(jnp.float32).reshape(GROUPS, tokens, blocks, BLOCK)
    rotated = jnp.einsum('gtbk,kj->gtbj', pieces, table, precision=lax.Precision.HIGHEST)
    scale = lax.optimization_barrier(jnp.mean(jnp.abs(rotated), axis=-1)) + 1e-06
    coded = jnp.clip(rotated / scale[..., None], -code_limit, code_limit).astype(jnp.bfloat16)
    summed = lax.optimization_barrier(jnp.sum(coded.astype(jnp.float32) * scale[..., None], axis=0))
    rescale = lax.optimization_barrier(jnp.mean(jnp.abs(summed), axis=-1)) + 1e-06
    recoded = jnp.clip(summed / rescale[..., None], -code_limit, code_limit).astype(jnp.bfloat16)
    back = jnp.einsum('tbk,kj->tbj', recoded.astype(jnp.float32), table, precision=lax.Precision.HIGHEST)
    back = back * (rescale / BLOCK)[..., None]
    return (flat + back.reshape(tokens, width)).astype(jnp.bfloat16)

def reference(hidden, norm_gain, q_gain, out_weight, positions):
    table = sign_table(BLOCK)
    state = hidden
    pos = positions
    for tick in range(TICKS):
        state = lax.map(lambda operands: section_layer(table, operands), (state, norm_gain, q_gain, out_weight, pos))
        state = jnp.roll(state, 1, axis=0)
        pos = jnp.roll(pos, 1, axis=0)
    return state
```

```python
import jax
import jax.numpy as jnp
from jax import lax
from jax.experimental import pallas as pl
from jax.experimental.pallas import tpu as pltpu
from jax.sharding import PartitionSpec as P

MESH = pl.DeviceIdType.MESH
F32 = jnp.float32
BF16 = jnp.bfloat16
HEAD = 128
BLOCK = 128
TICKS = 2
LIMIT = 3.0
NZ = 16
TILE = 256
TOK = 128
ROWS = 8
HALF = 2048
NSUB = 4
PART = HALF // NSUB


def constants():
    rows = lax.broadcasted_iota(jnp.int32, (TILE, TILE), 0)
    cols = lax.broadcasted_iota(jnp.int32, (TILE, TILE), 1)
    same = jnp.right_shift(rows, 7) == jnp.right_shift(cols, 7)
    both = jnp.bitwise_and(rows, cols)
    for shift in (4, 2, 1):
        both = jnp.bitwise_xor(both, jnp.right_shift(both, shift)) if shift != 4 else jnp.bitwise_xor(
            jnp.bitwise_and(both, 15), jnp.bitwise_and(jnp.right_shift(both, 4), 7)
        )
    sign = (1 - 2 * jnp.bitwise_and(both, 1)).astype(F32)
    signs = jnp.where(same, sign, 0.0).astype(BF16)
    means = jnp.where(same, 1.0 / BLOCK, 0.0).astype(BF16)
    return signs, means


def swap(p, q):
    low = lax.broadcasted_iota(jnp.int32, p.shape, 0) < 4
    return (
        jnp.where(low, p, pltpu.roll(q, 4, 0)),
        jnp.where(low, pltpu.roll(p, 4, 0), q),
    )


def dot(a, b):
    return jnp.dot(a, b, preferred_element_type=F32)


def kernel(
    hidden, gain, qgain, weight, pos, out,
    signs, means, x8, st, wb, msb, mrb, gbuf, pbuf, asb, arb, cbuf, terms, sb, rb, ssb, srb, rsb, rrb, fsb, frb,
    wsem, wss, wrs, mss, mrs, ass, ars, css, crs, rss, rrs, fss, frs,
):
    sec = lax.axis_index("section")
    tp = lax.axis_index("tp")
    nsec = lax.axis_size("section")
    z = tp // 2
    k = lax.rem(tp, 2)
    sib = (sec, z * 2 + 1 - k)
    nxt = lax.rem(sec + 1, nsec)
    prv = lax.rem(sec + nsec - 1, nsec)

    def far(i):
        return lax.rem(z + i, NZ)

    def remote(src, dst, send, recv, device):
        return pltpu.make_async_remote_copy(
            src_ref=src, dst_ref=dst, send_sem=send, recv_sem=recv, device_id=device, device_id_type=MESH
        )

    def wcols(jj, parity):
        return pl.ds(pl.multiple_of((2 * jj + parity) * TILE, TILE), TILE)

    def wlocal(jj):
        return pltpu.make_async_copy(weight.at[0, :, wcols(jj, k)], wb.at[0, jj], wsem.at[jj])

    def wremote(jj):
        return remote(weight.at[0, :, wcols(jj, 1 - k)], wb.at[1, jj], wss.at[jj], wrs.at[jj], sib)

    def loop(n, body):
        lax.fori_loop(0, n, lambda i, c: (body(i), c)[1], 0)

    loop(NZ, lambda jj: wlocal(jj).start())

    barrier = pltpu.get_barrier_semaphore()

    def greet(section, member):
        pl.semaphore_signal(barrier, inc=1, device_id=(section, member), device_id_type=MESH)

    def greet_far(i):
        greet(sec, far(i) * 2 + k)
        greet(prv, far(i) * 2 + k)

    greet(*sib)
    lax.fori_loop(1, NZ, lambda i, c: (greet_far(i), c)[1], 0)
    greet(prv, z * 2 + k)
    greet(prv, z * 2 + 1 - k)
    greet(nxt, z * 2 + k)

    sg, mn = constants()
    signs[...] = sg
    means[...] = mn

    x = hidden[0].astype(F32)
    x8[0:4, :] = x
    x8[4:8, :] = x
    x = x8[...]
    scale = lax.rsqrt(jnp.mean(x * x, axis=1, keepdims=True) + 1e-05)
    normed = x * scale * gain[...]

    def pack(v, parity):
        quarters = []
        for q in range(4):
            quarters.append(
                jnp.concatenate(
                    [v[:, (2 * jj + parity) * TILE : (2 * jj + parity + 1) * TILE] for jj in range(4 * q, 4 * q + 4)],
                    axis=1,
                )
            )
        return jnp.concatenate([swap(quarters[0], quarters[1])[0], swap(quarters[2], quarters[3])[0]], axis=0)

    even = k == 0
    for i, v in enumerate((normed, x)):
        p0, p1 = pack(v, 0), pack(v, 1)
        msb[i] = jnp.where(even, p0, p1).astype(BF16)
        msb[2 + i] = jnp.where(even, p1, p0).astype(BF16)

    pl.semaphore_wait(barrier, 2 * NZ + 2)

    packs = [remote(msb.at[2 + i], mrb.at[i], mss.at[i], mrs.at[i], sib) for i in range(2)]
    for c in packs:
        c.start()
    loop(NZ, lambda jj: wremote(jj).start())
    gains = remote(gain, gbuf, mss.at[2], mrs.at[2], (prv, z * 2 + k))
    gains.start()
    places = remote(pos, pbuf, mss.at[3], mrs.at[3], (nxt, z * 2 + k))
    places.start()

    def unpack(i):
        mine, other = msb[i].astype(F32), mrb[i].astype(F32)
        a = jnp.where(even, mine, other)
        b = jnp.where(even, other, mine)
        halves = [jnp.concatenate(swap(a[8 * h : 8 * h + 8], b[8 * h : 8 * h + 8]), axis=1) for h in range(2)]
        return jnp.concatenate(halves, axis=0)

    def a2a_copy(tick, i):
        j = far(i)
        return remote(
            asb.at[tick, j], arb.at[tick, z], ass.at[tick, j], ars.at[tick, z],
            (sec if tick == 0 else nxt, j * 2 + k),
        )

    def a2a_recv(tick, i):
        j = far(i)
        return remote(asb.at[tick, j], arb.at[tick, j], ass.at[tick, j], ars.at[tick, j], (sec, j * 2 + k))

    def spread(tick, rows):
        for jj in range(NZ):
            h, c = jj // 8, (jj % 8) * TILE
            asb[tick, jj] = jnp.concatenate(
                [rows[8 * h : 8 * h + 8, c : c + HEAD], rows[8 * h : 8 * h + 8, c + HEAD : c + 2 * HEAD]], axis=0
            ).astype(BF16)
        lax.fori_loop(0 if tick else 1, NZ, lambda i, c: (a2a_copy(tick, lax.rem(i + 8, NZ) if tick else i).start(), c)[1], 0)
        if tick == 0:
            arb[0, z] = asb[0, z]

    packs[0].wait_recv()
    spread(0, unpack(0))
    packs[1].wait_recv()
    st[...] = unpack(1)

    def rotate(g):
        def one(jj):
            if g == 0:
                wlocal(jj).wait()
            else:
                wremote(jj).wait_recv()
            wb[g, jj] = dot(wb[g, jj], signs[...]).astype(BF16)

        loop(NZ, one)

    rotate(0)
    rotate(1)

    def attend(tick):
        rid = lax.broadcasted_iota(jnp.int32, (TOK, TOK), 0)
        cid = lax.broadcasted_iota(jnp.int32, (TOK, TOK), 1)
        row = (pos if tick == 0 else pbuf)[...].astype(F32)
        back = jnp.sum(jnp.where(rid == cid, jnp.broadcast_to(row, (TOK, TOK)), 0.0), axis=1, keepdims=True)
        seen = (cid <= rid) & (cid.astype(F32) >= rid.astype(F32) - back)
        lax.fori_loop(0 if tick else 1, NZ, lambda i, c: (a2a_recv(tick, i).wait_recv(), c)[1], 0)
        v = arb[tick].astype(F32).reshape(NZ, 2, ROWS, HEAD)
        for h in range(2):
            keys = v[:, h].reshape(TOK, HEAD)
            qg = qgain[:, pl.ds(pl.multiple_of(tp * TILE + h * HEAD, HEAD), HEAD)]
            query = (keys * qg).astype(BF16)
            keys = keys.astype(BF16)
            scores = lax.dot_general(query, keys, (((1,), (1,)), ((), ())), preferred_element_type=F32) * HEAD ** (-0.5)
            scores = jnp.where(seen, scores, -1e30)
            top = jnp.max(scores, axis=1, keepdims=True)
            expo = jnp.where(seen, jnp.exp(scores - top), 0.0)
            weights = (expo / jnp.sum(expo, axis=1, keepdims=True)).astype(BF16)
            cbuf[tick, 0, :, h * HEAD : (h + 1) * HEAD] = dot(weights, keys).astype(BF16)

    def part_terms(tick, j):
        for h in range(2):
            for i in range(PART // TILE):
                jj = h * 8 + j * (PART // TILE) + i
                total = None
                for g in range(2):
                    rotated = dot(cbuf[tick, g], wb[g, jj])
                    bound = dot(jnp.abs(rotated).astype(BF16), means[...]) * LIMIT + LIMIT * 1e-06
                    term = jnp.clip(rotated, -bound, bound)
                    total = term if total is None else total + term
                terms[:, h * 8 : h * 8 + 8, j * PART + i * TILE : j * PART + (i + 1) * TILE] = total.reshape(NZ, ROWS, TILE)

    def chain(tick, t, d, j):
        cols = pl.ds(j * PART, PART)
        to = (sec, far(1 if d == 0 else NZ - 1) * 2 + k)
        return remote(
            sb.at[tick, t, d, :, cols], rb.at[tick, t, d, :, cols], rss.at[tick, t, d, j], rrs.at[tick, t, d, j], to
        )

    def starts(t, d, j):
        return t == 0 or (t == 1 and j % 2 != d)

    def reduce(tick):
        for t in range(8):
            for j in range(NSUB):
                if t == 0:
                    part_terms(tick, j)
                cols = slice(j * PART, (j + 1) * PART)
                for d in range(2):
                    if t == 0 and j % 2 != d:
                        continue
                    owner = far(8 - t if d == 0 else 8 + t)
                    v = terms[owner, :, cols]
                    if not starts(t, d, j):
                        chain(tick, t - 1, d, j).wait_recv()
                        v = v + rb[tick, t - 1, d, :, cols].astype(F32)
                    sb[tick, t, d, :, cols] = v.astype(BF16)
                    chain(tick, t, d, j).start()
        sums = []
        for j in range(NSUB):
            cols = slice(j * PART, (j + 1) * PART)
            for d in range(2):
                chain(tick, 7, d, j).wait_recv()
            sums.append(terms[z, :, cols] + rb[tick, 7, 0, :, cols].astype(F32) + rb[tick, 7, 1, :, cols].astype(F32))
        summed = jnp.concatenate(sums, axis=1)
        n = HALF // BLOCK
        tall = jnp.concatenate([summed[:, b * BLOCK : (b + 1) * BLOCK] for b in range(n)], axis=0)
        rescale = jnp.mean(jnp.abs(tall), axis=1, keepdims=True) + 1e-06
        recoded = jnp.clip(tall / rescale, -LIMIT, LIMIT).astype(BF16)
        back = dot(recoded, signs[0:BLOCK, 0:BLOCK]) * (rescale / BLOCK)
        wide = jnp.concatenate([back[b * 16 : (b + 1) * 16] for b in range(n)], axis=1)
        return (st[...] + wide).astype(BF16)

    for tick in range(TICKS):
        attend(tick)
        swapc = remote(cbuf.at[tick, 0], cbuf.at[tick, 1], css.at[tick], crs.at[tick], sib)
        swapc.start()
        swapc.wait_recv()
        rows = reduce(tick)
        if tick == 0:
            state = rows.astype(F32)
            rsb[...] = rows
            part = jnp.sum(state * state, axis=1, keepdims=True)
            part = part[0:8] + part[8:16]
            ssb[...] = jnp.broadcast_to(part, (ROWS, BLOCK))
            sums = remote(ssb, srb, mss.at[4], mrs.at[4], sib)
            sums.start()
            residual = remote(rsb, rrb, mss.at[5], mrs.at[5], (nxt, z * 2 + k))
            residual.start()
            gains.wait_recv()
            cut = [gbuf[:, wcols(jj, k)] for jj in range(NZ)]
            sums.wait_recv()
            scale = lax.rsqrt((ssb[:, 0:1] + srb[:, 0:1]) / (2.0 * 2 * HALF) + 1e-05)
            halves = [
                state[8 * h : 8 * h + 8] * scale * jnp.concatenate(cut[8 * h : 8 * h + 8], axis=1) for h in range(2)
            ]
            spread(1, jnp.concatenate(halves, axis=0))
            places.wait_recv()
            residual.wait_recv()
            st[...] = rrb[...].astype(F32)
        else:
            v = rows.astype(F32)
            pair = [swap(v[8 * h : 8 * h + 8, 0:1024], v[8 * h : 8 * h + 8, 1024:2048]) for h in range(2)]
            for c in range(2):
                fsb[c] = jnp.concatenate([pair[0][c], pair[1][c]], axis=0).astype(BF16)

    def final(c):
        return remote(fsb.at[c], frb.at[k], fss.at[c], frs.at[k], (nxt, z * 2 + c))

    for c in range(2):
        final(c).start()
    for c in range(2):
        remote(fsb.at[c], frb.at[c], fss.at[c], frs.at[c], (nxt, z * 2 + c)).wait_recv()
    got = [frb[c].astype(F32) for c in range(2)]
    pieces = []
    for jj in range(NZ):
        q, c0 = jj // 4, (jj % 4) * TILE
        for c in range(2):
            v = got[c][8 * (q // 2) : 8 * (q // 2) + 8, c0 : c0 + TILE]
            pieces.append(pltpu.roll(v, 4, 0) if q % 2 else v)
    out[0] = jnp.concatenate(pieces, axis=1)[0:4].astype(BF16)

    for c in packs + [gains, places, sums, residual]:
        c.wait_send()
    loop(NZ, lambda jj: wremote(jj).wait_send())
    for tick in range(TICKS):
        lax.fori_loop(0 if tick else 1, NZ, lambda i, c: (a2a_copy(tick, i).wait_send(), c)[1], 0)
        remote(cbuf.at[tick, 0], cbuf.at[tick, 1], css.at[tick], crs.at[tick], sib).wait_send()
        for t in range(8):
            for j in range(NSUB):
                for d in range(2):
                    if t == 0 and j % 2 != d:
                        continue
                    chain(tick, t, d, j).wait_send()
    for c in range(2):
        final(c).wait_send()


def per_device(hidden, norm_gain, q_gain, out_weight, positions):
    vmem = pl.BlockSpec(memory_space=pltpu.VMEM)
    dma = pltpu.SemaphoreType.DMA
    return pl.pallas_call(
        kernel,
        out_shape=jax.ShapeDtypeStruct(hidden.shape, BF16),
        in_specs=[vmem, vmem, vmem, pl.BlockSpec(memory_space=pl.ANY), vmem],
        out_specs=vmem,
        scratch_shapes=[
            pltpu.VMEM((TILE, TILE), BF16),
            pltpu.VMEM((TILE, TILE), BF16),
            pltpu.VMEM((8, 8192), F32),
            pltpu.VMEM((16, HALF), F32),
            pltpu.VMEM((2, NZ, TILE, TILE), BF16),
            pltpu.VMEM((4, 16, 1024), BF16),
            pltpu.VMEM((2, 16, 1024), BF16),
            pltpu.VMEM((1, 8192), F32),
            pltpu.VMEM((1, TOK), jnp.int32),
            pltpu.VMEM((2, NZ, 16, HEAD), BF16),
            pltpu.VMEM((2, NZ, 16, HEAD), BF16),
            pltpu.VMEM((2, 2, TOK, TILE), BF16),
            pltpu.VMEM((NZ, 16, HALF), F32),
            pltpu.VMEM((2, 8, 2, 16, HALF), BF16),
            pltpu.VMEM((2, 8, 2, 16, HALF), BF16),
            pltpu.VMEM((ROWS, BLOCK), F32),
            pltpu.VMEM((ROWS, BLOCK), F32),
            pltpu.VMEM((16, HALF), BF16),
            pltpu.VMEM((16, HALF), BF16),
            pltpu.VMEM((2, 16, 1024), BF16),
            pltpu.VMEM((2, 16, 1024), BF16),
            dma((NZ,)),
            dma((NZ,)),
            dma((NZ,)),
            dma((6,)),
            dma((6,)),
            dma((2, NZ)),
            dma((2, NZ)),
            dma((2,)),
            dma((2,)),
            dma((2, 8, 2, NSUB)),
            dma((2, 8, 2, NSUB)),
            dma((2,)),
            dma((2,)),
        ],
        compiler_params=pltpu.CompilerParams(
            collective_id=0, has_side_effects=True, vmem_limit_bytes=40 * 1024 * 1024
        ),
    )(hidden, norm_gain, q_gain, out_weight, positions)


def solution(mesh):
    return jax.shard_map(
        per_device,
        mesh=mesh,
        in_specs=(
            P("section", "tp", None),
            P("section", None),
            P("section", None),
            P("section", "tp", None),
            P("section", None),
        ),
        out_specs=P("section", "tp", None),
        check_vma=False,
    )
```

```python
import jax
import jax.numpy as jnp
from jax import lax
from jax.experimental import pallas as pl
from jax.experimental.pallas import tpu as pltpu
from jax.sharding import PartitionSpec as P

MESH = pl.DeviceIdType.MESH
F32 = jnp.float32
BF16 = jnp.bfloat16
HEAD = 128
BLOCK = 128
TICKS = 2
LIMIT = 3.0
NZ = 16
TILE = 256
TOK = 128
ROWS = 8
HALF = 2048
NSUB = 4
PART = HALF // NSUB
NEAR = 4


def constants():
    rows = lax.broadcasted_iota(jnp.int32, (TILE, TILE), 0)
    cols = lax.broadcasted_iota(jnp.int32, (TILE, TILE), 1)
    same = jnp.right_shift(rows, 7) == jnp.right_shift(cols, 7)
    both = jnp.bitwise_and(rows, cols)
    for shift in (4, 2, 1):
        both = jnp.bitwise_xor(both, jnp.right_shift(both, shift)) if shift != 4 else jnp.bitwise_xor(
            jnp.bitwise_and(both, 15), jnp.bitwise_and(jnp.right_shift(both, 4), 7)
        )
    sign = (1 - 2 * jnp.bitwise_and(both, 1)).astype(F32)
    signs = jnp.where(same, sign, 0.0).astype(BF16)
    means = jnp.where(same, 1.0 / BLOCK, 0.0).astype(BF16)
    return signs, means


def swap(p, q):
    low = lax.broadcasted_iota(jnp.int32, p.shape, 0) < 4
    return (
        jnp.where(low, p, pltpu.roll(q, 4, 0)),
        jnp.where(low, pltpu.roll(p, 4, 0), q),
    )


def dot(a, b):
    return jnp.dot(a, b, preferred_element_type=F32)


def kernel(
    hidden_hbm, gain_hbm, qgain_hbm, weight, pos_hbm, out,
    hidden, gain, qgain, pos,
    signs, means, x8, st, wb, msb, mrb, gbuf, pbuf, asb, arb, cbuf, terms, sb, rb, ssb, srb, rsb, rrb, fsb, frb,
    lsem, wsem, wss, wrs, mss, mrs, ass, ars, css, crs, rss, rrs, fss, frs,
):
    sec = lax.axis_index("section")
    tp = lax.axis_index("tp")
    nsec = lax.axis_size("section")
    z = tp // 2
    k = lax.rem(tp, 2)
    sib = (sec, z * 2 + 1 - k)
    nxt = lax.rem(sec + 1, nsec)
    prv = lax.rem(sec + nsec - 1, nsec)

    def far(i):
        return lax.rem(z + i, NZ)

    def farthest(n):
        half = (n + 1) // 2
        return far(NZ // 2 + half * (1 - 2 * lax.rem(n, 2)) + NZ)

    def remote(src, dst, send, recv, device):
        return pltpu.make_async_remote_copy(
            src_ref=src, dst_ref=dst, send_sem=send, recv_sem=recv, device_id=device, device_id_type=MESH
        )

    def wcols(jj, parity):
        return pl.ds(pl.multiple_of((2 * jj + parity) * TILE, TILE), TILE)

    def wlocal(jj):
        return pltpu.make_async_copy(weight.at[0, :, wcols(jj, k)], wb.at[0, jj], wsem.at[jj])

    def wremote(jj):
        return remote(weight.at[0, :, wcols(jj, 1 - k)], wb.at[1, jj], wss.at[jj], wrs.at[jj], sib)

    def loop(n, body):
        lax.fori_loop(0, n, lambda i, c: (body(i), c)[1], 0)

    barrier = pltpu.get_barrier_semaphore()

    def greet(section, member):
        pl.semaphore_signal(barrier, inc=1, device_id=(section, member), device_id_type=MESH)

    def greet_far(n):
        greet(sec, farthest(n) * 2 + k)
        greet(prv, farthest(n) * 2 + k)

    loop(NZ - 1, greet_far)
    greet(*sib)
    greet(prv, z * 2 + k)
    greet(prv, z * 2 + 1 - k)
    greet(nxt, z * 2 + k)

    loads = [
        pltpu.make_async_copy(src, dst, lsem.at[i])
        for i, (src, dst) in enumerate(
            ((hidden_hbm, hidden), (gain_hbm, gain), (pos_hbm, pos), (qgain_hbm, qgain))
        )
    ]
    for c in loads:
        c.start()
    loop(NZ, lambda jj: wlocal(jj).start())

    sg, mn = constants()
    signs[...] = sg
    means[...] = mn

    loads[0].wait()
    x = hidden[0].astype(F32)
    x8[0:4, :] = x
    x8[4:8, :] = x
    x = x8[...]
    scale = lax.rsqrt(jnp.mean(x * x, axis=1, keepdims=True) + 1e-05)
    loads[1].wait()
    normed = x * scale * gain[...]

    def pack(v, parity):
        quarters = []
        for q in range(4):
            quarters.append(
                jnp.concatenate(
                    [v[:, (2 * jj + parity) * TILE : (2 * jj + parity + 1) * TILE] for jj in range(4 * q, 4 * q + 4)],
                    axis=1,
                )
            )
        return jnp.concatenate([swap(quarters[0], quarters[1])[0], swap(quarters[2], quarters[3])[0]], axis=0)

    even = k == 0
    for i, v in enumerate((normed, x)):
        p0, p1 = pack(v, 0), pack(v, 1)
        msb[i] = jnp.where(even, p0, p1).astype(BF16)
        msb[2 + i] = jnp.where(even, p1, p0).astype(BF16)

    loads[2].wait()
    loads[3].wait()
    pl.semaphore_wait(barrier, 2 * NZ + 2)

    packs = [remote(msb.at[2 + i], mrb.at[i], mss.at[i], mrs.at[i], sib) for i in range(2)]
    for c in packs:
        c.start()
    loop(NZ, lambda jj: wremote(jj).start())
    gains = remote(gain, gbuf, mss.at[2], mrs.at[2], (prv, z * 2 + k))
    gains.start()
    places = remote(pos, pbuf, mss.at[3], mrs.at[3], (nxt, z * 2 + k))
    places.start()

    def unpack(i):
        mine, other = msb[i].astype(F32), mrb[i].astype(F32)
        a = jnp.where(even, mine, other)
        b = jnp.where(even, other, mine)
        halves = [jnp.concatenate(swap(a[8 * h : 8 * h + 8], b[8 * h : 8 * h + 8]), axis=1) for h in range(2)]
        return jnp.concatenate(halves, axis=0)

    def a2a_copy(tick, n):
        j = farthest(n)
        return remote(
            asb.at[tick, j], arb.at[tick, z], ass.at[tick, j], ars.at[tick, z],
            (sec if tick == 0 else nxt, j * 2 + k),
        )

    def a2a_recv(tick, n):
        j = farthest(n)
        return remote(asb.at[tick, j], arb.at[tick, j], ass.at[tick, j], ars.at[tick, j], (sec, j * 2 + k))

    def spread(tick, rows):
        for jj in range(NZ):
            h, c = jj // 8, (jj % 8) * TILE
            asb[tick, jj] = jnp.concatenate(
                [rows[8 * h : 8 * h + 8, c : c + HEAD], rows[8 * h : 8 * h + 8, c + HEAD : c + 2 * HEAD]], axis=0
            ).astype(BF16)
        loop(NZ - 1 + tick, lambda n: a2a_copy(tick, n).start())
        if tick == 0:
            arb[0, z] = asb[0, z]

    packs[0].wait_recv()
    spread(0, unpack(0))
    packs[1].wait_recv()
    st[...] = unpack(1)

    def rotate(g, jj):
        if g == 0:
            wlocal(jj).wait()
        else:
            wremote(jj).wait_recv()
        wb[g, jj] = dot(wb[g, jj], signs[...]).astype(BF16)

    loop(NZ, lambda jj: rotate(0, jj))

    def attend(tick):
        rid = lax.broadcasted_iota(jnp.int32, (TOK, TOK), 0)
        cid = lax.broadcasted_iota(jnp.int32, (TOK, TOK), 1)
        row = (pos if tick == 0 else pbuf)[...].astype(F32)
        back = jnp.sum(jnp.where(rid == cid, jnp.broadcast_to(row, (TOK, TOK)), 0.0), axis=1, keepdims=True)
        seen = (cid <= rid) & (cid.astype(F32) >= rid.astype(F32) - back)
        loop(NZ - 1 + tick, lambda n: a2a_recv(tick, NZ - 2 + tick - n).wait_recv())
        v = arb[tick].astype(F32).reshape(NZ, 2, ROWS, HEAD)
        for h in range(2):
            keys = v[:, h].reshape(TOK, HEAD)
            qg = qgain[:, pl.ds(pl.multiple_of(tp * TILE + h * HEAD, HEAD), HEAD)]
            query = (keys * qg).astype(BF16)
            keys = keys.astype(BF16)
            scores = lax.dot_general(query, keys, (((1,), (1,)), ((), ())), preferred_element_type=F32) * HEAD ** (-0.5)
            scores = jnp.where(seen, scores, -1e30)
            top = jnp.max(scores, axis=1, keepdims=True)
            expo = jnp.where(seen, jnp.exp(scores - top), 0.0)
            weights = (expo / jnp.sum(expo, axis=1, keepdims=True)).astype(BF16)
            cbuf[tick, 0, :, h * HEAD : (h + 1) * HEAD] = dot(weights, keys).astype(BF16)

    def swap_context(tick):
        return remote(cbuf.at[tick, 0], cbuf.at[tick, 1], css.at[tick], crs.at[tick], sib)

    def part_terms(tick, j):
        n = PART // TILE
        for g in range(2):
            if g == 1 and j == 0:
                swap_context(tick).wait_recv()
            if g == 1 and tick == 0:
                for h in range(2):
                    for i in range(n):
                        rotate(1, h * 8 + j * n + i)
            for h in range(2):
                for i in range(n):
                    place = (slice(None), slice(h * 8, h * 8 + 8), slice(j * PART + i * TILE, j * PART + (i + 1) * TILE))
                    rotated = dot(cbuf[tick, g], wb[g, h * 8 + j * n + i])
                    bound = dot(jnp.abs(rotated).astype(BF16), means[...]) * LIMIT + LIMIT * 1e-06
                    term = jnp.clip(rotated, -bound, bound).reshape(NZ, ROWS, TILE)
                    terms[place] = term if g == 0 else terms[place] + term

    def chain(tick, dist, d, j):
        hops = dist if dist == NEAR + 1 else 1
        to = (sec, far(hops if d == 0 else NZ - hops) * 2 + k)
        cols = pl.ds(j * PART, PART)
        return remote(
            sb.at[tick, dist - 1, d, :, cols], rb.at[tick, dist - 1, d, :, cols],
            rss.at[tick, dist - 1, d, j], rrs.at[tick, dist - 1, d, j], to,
        )

    def step(tick, dist, d, j):
        if dist == 8 and j % 2 != d:
            return
        cols = slice(j * PART, (j + 1) * PART)
        v = terms[far(dist if d == 0 else NZ - dist), :, cols]
        if not (dist in (8, NEAR) or (dist == 7 and j % 2 != d)):
            chain(tick, dist + 1, d, j).wait_recv()
            v = v + rb[tick, dist, d, :, cols].astype(F32)
        sb[tick, dist - 1, d, :, cols] = v.astype(BF16)
        chain(tick, dist, d, j).start()

    def chain_sent(tick):
        def one(q):
            for j in range(NSUB):
                cols = pl.ds(j * PART, PART)
                src = sb.at[tick, q // 2, lax.rem(q, 2), :, cols]
                remote(
                    src, rb.at[tick, q // 2, lax.rem(q, 2), :, cols],
                    rss.at[tick, q // 2, lax.rem(q, 2), j], rrs.at[tick, q // 2, lax.rem(q, 2), j], sib,
                ).wait_send()

        loop(14, one)
        for j in range(NSUB):
            chain(tick, 8, j % 2, j).wait_send()

    def reduce(tick):
        for j in range(NSUB):
            part_terms(tick, j)
            for dist in (8, NEAR):
                for d in range(2):
                    step(tick, dist, d, j)
        for t in range(1, 8 - NEAR):
            for dist in (8 - t, NEAR - t):
                for j in range(NSUB):
                    for d in range(2):
                        step(tick, dist, d, j)

    def restore(tick, j):
        cols = slice(j * PART, (j + 1) * PART)
        summed = terms[z, :, cols]
        for dist in (1, NEAR + 1):
            for d in range(2):
                chain(tick, dist, d, j).wait_recv()
                summed = summed + rb[tick, dist - 1, d, :, cols].astype(F32)
        n = PART // BLOCK
        tall = jnp.concatenate([summed[:, b * BLOCK : (b + 1) * BLOCK] for b in range(n)], axis=0)
        rescale = jnp.mean(jnp.abs(tall), axis=1, keepdims=True) + 1e-06
        recoded = jnp.clip(tall / rescale, -LIMIT, LIMIT).astype(BF16)
        back = dot(recoded, signs[0:BLOCK, 0:BLOCK]) * (rescale / BLOCK)
        wide = jnp.concatenate([back[b * 16 : (b + 1) * 16] for b in range(n)], axis=1)
        return (st[:, cols] + wide).astype(BF16)

    def final(c, j):
        cols = pl.ds(j * TILE, TILE)
        return remote(
            fsb.at[c, :, cols], frb.at[k, :, cols], fss.at[c, j], frs.at[k, j], (nxt, z * 2 + c)
        )

    attend(0)
    swap_context(0).start()
    reduce(0)
    part = None
    for j in range(NSUB):
        rows = restore(0, j)
        cols = slice(j * PART, (j + 1) * PART)
        rsb[:, cols] = rows
        wide = rows.astype(F32)
        squares = jnp.sum(wide * wide, axis=1, keepdims=True)
        part = squares if part is None else part + squares
    ssb[...] = jnp.broadcast_to(part[0:8] + part[8:16], (ROWS, BLOCK))
    sums = remote(ssb, srb, mss.at[4], mrs.at[4], sib)
    sums.start()
    gains.wait_recv()
    state = rsb[...].astype(F32)
    scaled = jnp.concatenate(
        [
            state[8 * h : 8 * h + 8] * jnp.concatenate([gbuf[:, wcols(8 * h + i, k)] for i in range(8)], axis=1)
            for h in range(2)
        ],
        axis=0,
    )
    sums.wait_recv()
    scale = lax.rsqrt((ssb[:, 0:1] + srb[:, 0:1]) / (2.0 * 2 * HALF) + 1e-05)
    spread(1, scaled * jnp.concatenate([scale, scale], axis=0))
    residual = remote(rsb, rrb, mss.at[5], mrs.at[5], (nxt, z * 2 + k))
    residual.start()

    for c in packs + [gains, places, sums]:
        c.wait_send()
    loop(NZ, lambda jj: wremote(jj).wait_send())
    loop(NZ - 1, lambda n: a2a_copy(0, n).wait_send())
    swap_context(0).wait_send()
    chain_sent(0)
    places.wait_recv()

    attend(1)
    swap_context(1).start()
    reduce(1)
    residual.wait_recv()
    st[...] = rrb[...].astype(F32)
    for j in range(NSUB):
        v = restore(1, j).astype(F32)
        pair = [swap(v[8 * h : 8 * h + 8, 0:TILE], v[8 * h : 8 * h + 8, TILE:PART]) for h in range(2)]
        for c in range(2):
            fsb[c, :, j * TILE : (j + 1) * TILE] = jnp.concatenate([pair[0][c], pair[1][c]], axis=0).astype(BF16)
            final(c, j).start()

    residual.wait_send()
    loop(NZ, lambda n: a2a_copy(1, n).wait_send())
    swap_context(1).wait_send()
    chain_sent(1)
    for c in range(2):
        for j in range(NSUB):
            cols = pl.ds(j * TILE, TILE)
            remote(
                fsb.at[c, :, cols], frb.at[c, :, cols], fss.at[c, j], frs.at[c, j], (nxt, z * 2 + c)
            ).wait_recv()
    got = [frb[c].astype(F32) for c in range(2)]
    pieces = []
    for jj in range(NZ):
        h, j = jj // 8, (jj % 8) // 2
        for c in range(2):
            v = got[c][8 * h : 8 * h + 8, j * TILE : (j + 1) * TILE]
            pieces.append(pltpu.roll(v, 4, 0) if jj % 2 else v)
    out[0] = jnp.concatenate(pieces, axis=1)[0:4].astype(BF16)
    for c in range(2):
        for j in range(NSUB):
            final(c, j).wait_send()


def per_device(hidden, norm_gain, q_gain, out_weight, positions):
    vmem = pl.BlockSpec(memory_space=pltpu.VMEM)
    dma = pltpu.SemaphoreType.DMA
    return pl.pallas_call(
        kernel,
        out_shape=jax.ShapeDtypeStruct(hidden.shape, BF16),
        in_specs=[pl.BlockSpec(memory_space=pltpu.HBM)] * 5,
        out_specs=vmem,
        scratch_shapes=[
            pltpu.VMEM((1, 4, 8192), BF16),
            pltpu.VMEM((1, 8192), F32),
            pltpu.VMEM((1, 8192), F32),
            pltpu.VMEM((1, TOK), jnp.int32),
            pltpu.VMEM((TILE, TILE), BF16),
            pltpu.VMEM((TILE, TILE), BF16),
            pltpu.VMEM((8, 8192), F32),
            pltpu.VMEM((16, HALF), F32),
            pltpu.VMEM((2, NZ, TILE, TILE), BF16),
            pltpu.VMEM((4, 16, 1024), BF16),
            pltpu.VMEM((2, 16, 1024), BF16),
            pltpu.VMEM((1, 8192), F32),
            pltpu.VMEM((1, TOK), jnp.int32),
            pltpu.VMEM((2, NZ, 16, HEAD), BF16),
            pltpu.VMEM((2, NZ, 16, HEAD), BF16),
            pltpu.VMEM((2, 2, TOK, TILE), BF16),
            pltpu.VMEM((NZ, 16, HALF), F32),
            pltpu.VMEM((2, 8, 2, 16, HALF), BF16),
            pltpu.VMEM((2, 8, 2, 16, HALF), BF16),
            pltpu.VMEM((ROWS, BLOCK), F32),
            pltpu.VMEM((ROWS, BLOCK), F32),
            pltpu.VMEM((16, HALF), BF16),
            pltpu.VMEM((16, HALF), BF16),
            pltpu.VMEM((2, 16, 1024), BF16),
            pltpu.VMEM((2, 16, 1024), BF16),
            dma((4,)),
            dma((NZ,)),
            dma((NZ,)),
            dma((NZ,)),
            dma((6,)),
            dma((6,)),
            dma((2, NZ)),
            dma((2, NZ)),
            dma((2,)),
            dma((2,)),
            dma((2, 8, 2, NSUB)),
            dma((2, 8, 2, NSUB)),
            dma((2, NSUB)),
            dma((2, NSUB)),
        ],
        compiler_params=pltpu.CompilerParams(
            collective_id=0, has_side_effects=True, vmem_limit_bytes=60 * 1024 * 1024
        ),
    )(hidden, norm_gain, q_gain, out_weight, positions)


def solution(mesh):
    return jax.shard_map(
        per_device,
        mesh=mesh,
        in_specs=(
            P("section", "tp", None),
            P("section", None),
            P("section", None),
            P("section", "tp", None),
            P("section", None),
        ),
        out_specs=P("section", "tp", None),
        check_vma=False,
    )
```

```python
import jax
import jax.numpy as jnp
from jax import lax
from jax.experimental import pallas as pl
from jax.experimental.pallas import tpu as pltpu
from jax.sharding import PartitionSpec as P

MESH = pl.DeviceIdType.MESH
F32 = jnp.float32
BF16 = jnp.bfloat16
HEAD = 128
BLOCK = 128
TICKS = 2
LIMIT = 3.0
NZ = 16
TILE = 256
TOK = 128
ROWS = 8
HALF = 2048
NSUB = 4
PART = HALF // NSUB
EARLY = 6
NEAR = 4


def constants():
    rows = lax.broadcasted_iota(jnp.int32, (TILE, TILE), 0)
    cols = lax.broadcasted_iota(jnp.int32, (TILE, TILE), 1)
    same = jnp.right_shift(rows, 7) == jnp.right_shift(cols, 7)
    both = jnp.bitwise_and(rows, cols)
    for shift in (4, 2, 1):
        both = jnp.bitwise_xor(both, jnp.right_shift(both, shift)) if shift != 4 else jnp.bitwise_xor(
            jnp.bitwise_and(both, 15), jnp.bitwise_and(jnp.right_shift(both, 4), 7)
        )
    sign = (1 - 2 * jnp.bitwise_and(both, 1)).astype(F32)
    signs = jnp.where(same, sign, 0.0).astype(BF16)
    means = jnp.where(same, 1.0 / BLOCK, 0.0).astype(BF16)
    return signs, means


def swap(p, q):
    low = lax.broadcasted_iota(jnp.int32, p.shape, 0) < 4
    return (
        jnp.where(low, p, pltpu.roll(q, 4, 0)),
        jnp.where(low, pltpu.roll(p, 4, 0), q),
    )


def dot(a, b):
    return jnp.dot(a, b, preferred_element_type=F32)


def kernel(
    hidden_hbm, gain_hbm, qgain_hbm, weight, pos_hbm, out,
    hidden, gain, qgain, pos,
    signs, means, x8, st, wb, msb, mrb, gbuf, pbuf, asb, arb, cbuf, terms, sb, rb, ssb, srb, rsb, rrb, fsb, frb, rly,
    lsem, wsem, wss, wrs, mss, mrs, ass, ars, css, crs, rss, rrs, fss, frs, pss, rlr, sqs, sqr,
):
    sec = lax.axis_index("section")
    tp = lax.axis_index("tp")
    nsec = lax.axis_size("section")
    z = tp // 2
    k = lax.rem(tp, 2)
    sib = (sec, z * 2 + 1 - k)
    nxt = lax.rem(sec + 1, nsec)
    prv = lax.rem(sec + nsec - 1, nsec)

    def far(i):
        return lax.rem(z + i, NZ)

    def farthest(n):
        half = (n + 1) // 2
        return far(NZ // 2 + half * (1 - 2 * lax.rem(n, 2)) + NZ)

    def remote(src, dst, send, recv, device):
        return pltpu.make_async_remote_copy(
            src_ref=src, dst_ref=dst, send_sem=send, recv_sem=recv, device_id=device, device_id_type=MESH
        )

    def wcols(jj, parity):
        return pl.ds(pl.multiple_of((2 * jj + parity) * TILE, TILE), TILE)

    def wlocal(jj):
        return pltpu.make_async_copy(weight.at[0, :, wcols(jj, k)], wb.at[0, jj], wsem.at[jj])

    def wremote(jj):
        return remote(weight.at[0, :, wcols(jj, 1 - k)], wb.at[1, jj], wss.at[jj], wrs.at[jj], sib)

    def loop(n, body):
        lax.fori_loop(0, n, lambda i, c: (body(i), c)[1], 0)

    barrier = pltpu.get_barrier_semaphore()

    def greet(section, member):
        pl.semaphore_signal(barrier, inc=1, device_id=(section, member), device_id_type=MESH)

    order = [8, 7, 9, 6, 10, 5, 11, 4, 12, 3, 13, 2, 14, 1, 15]
    relayed = [i for i in order if 4 < i < 12]

    def by_relay(source, i):
        return jnp.logical_and(source < EARLY, lax.rem(source + i, NZ) >= EARLY)

    for i in order:
        if i in relayed:
            pl.when(jnp.logical_not(by_relay(far(NZ - i), i)))(lambda i=i: greet(sec, far(NZ - i) * 2 + k))
        else:
            greet(sec, far(NZ - i) * 2 + k)
    greet(*sib)
    greet(prv, z * 2 + k)
    greet(prv, z * 2 + 1 - k)
    greet(nxt, z * 2 + k)
    direct = NZ - 1 + 4
    for i in relayed:
        direct = direct - by_relay(z, i).astype(jnp.int32)

    loads = [
        pltpu.make_async_copy(src, dst, lsem.at[i])
        for i, (src, dst) in enumerate(
            ((hidden_hbm, hidden), (gain_hbm, gain), (pos_hbm, pos), (qgain_hbm, qgain))
        )
    ]
    for c in loads:
        c.start()
    loop(NZ, lambda jj: wlocal(jj).start())

    loads[0].wait()
    x = hidden[0].astype(F32)
    x8[0:4, :] = x
    x8[4:8, :] = x
    x = x8[...]
    scale = lax.rsqrt(jnp.mean(x * x, axis=1, keepdims=True) + 1e-05)
    loads[1].wait()
    normed = x * scale * gain[...]

    def pack(v, parity):
        quarters = []
        for q in range(4):
            quarters.append(
                jnp.concatenate(
                    [v[:, (2 * jj + parity) * TILE : (2 * jj + parity + 1) * TILE] for jj in range(4 * q, 4 * q + 4)],
                    axis=1,
                )
            )
        return jnp.concatenate([swap(quarters[0], quarters[1])[0], swap(quarters[2], quarters[3])[0]], axis=0)

    even = k == 0

    def pack_both(i, v):
        p0, p1 = pack(v, 0), pack(v, 1)
        msb[i] = jnp.where(even, p0, p1).astype(BF16)
        msb[2 + i] = jnp.where(even, p1, p0).astype(BF16)

    pack_both(0, normed)
    pl.semaphore_wait(barrier, direct)
    packs = [remote(msb.at[2 + i], mrb.at[i], mss.at[i], mrs.at[i], sib) for i in range(2)]
    packs[0].start()
    pack_both(1, x)
    gains = remote(gain, gbuf, mss.at[2], mrs.at[2], (prv, z * 2 + k))
    places = remote(pos, pbuf, mss.at[3], mrs.at[3], (nxt, z * 2 + k))

    def unpack(i):
        mine, other = msb[i].astype(F32), mrb[i].astype(F32)
        a = jnp.where(even, mine, other)
        b = jnp.where(even, other, mine)
        halves = [jnp.concatenate(swap(a[8 * h : 8 * h + 8], b[8 * h : 8 * h + 8]), axis=1) for h in range(2)]
        return jnp.concatenate(halves, axis=0)

    def a2a_copy(tick, j):
        return remote(
            asb.at[tick, j], arb.at[tick, z], ass.at[tick, j], ars.at[tick, z],
            (sec if tick == 0 else nxt, j * 2 + k),
        )

    def a2a_recv(tick, n):
        j = farthest(n)
        return remote(asb.at[tick, j], arb.at[tick, j], ass.at[tick, j], ars.at[tick, j], (sec, j * 2 + k))

    def message(tick, jj, v):
        asb[tick, jj] = jnp.concatenate([v[:, 0:HEAD], v[:, HEAD:TILE]], axis=0).astype(BF16)

    def square_copy(n, c):
        j = farthest(n)
        return remote(ssb, srb.at[tp], sqs.at[j * 2 + c], sqr.at[tp], (nxt, j * 2 + c))

    def pass_copy(i):
        origin = far(NZ - 4 if i <= 8 else 4)
        to = (sec, lax.rem(origin + i, NZ) * 2 + k)
        return remote(rly.at[i - 5], arb.at[0, origin], pss.at[i - 5], ars.at[0, origin], to)

    def relay_copy(i):
        to = (sec, far(4 if i <= 8 else NZ - 4) * 2 + k)
        return remote(asb.at[0, far(i)], rly.at[i - 5], ass.at[0, far(i)], rlr.at[i - 5], to)

    def direct_copy(i):
        return remote(asb.at[0, far(i)], arb.at[0, z], ass.at[0, far(i)], ars.at[0, z], (sec, far(i) * 2 + k))

    def passes(i):
        return by_relay(far(NZ - 4 if i <= 8 else 4), i)

    def first_sends():
        for i in order:
            if i in relayed:
                pl.when(by_relay(z, i))(lambda i=i: relay_copy(i).start())
                pl.when(jnp.logical_not(by_relay(z, i)))(lambda i=i: direct_copy(i).start())
            else:
                direct_copy(i).start()
        arb[0, z] = asb[0, z]

        packs[1].start()
        loop(NZ, lambda jj: wremote(jj).start())
        loads[2].wait()
        loads[3].wait()
        gains.start()
        places.start()

        def hand_on(i):
            relay_copy(i).wait_recv()
            pass_copy(i).start()

        for i in relayed:
            pl.when(passes(i))(lambda i=i: hand_on(i))

    packs[0].wait_recv()
    rows = unpack(0)
    for jj in range(NZ):
        h, c = jj // 8, (jj % 8) * TILE
        message(0, jj, rows[8 * h : 8 * h + 8, c : c + TILE])
    first_sends()
    packs[1].wait_recv()
    st[...] = unpack(1)

    def rotate(g, quarter):
        places = [quarter * 4 + i for i in range(4)]
        for jj in places:
            if g == 0:
                wlocal(jj).wait()
            else:
                wremote(jj).wait_recv()
        for jj in places:
            wb[g, jj] = dot(wb[g, jj], signs[...]).astype(BF16)

    sg, mn = constants()
    signs[...] = sg
    means[...] = mn
    loop(4, lambda quarter: rotate(0, quarter))
    loop(4, lambda quarter: rotate(1, quarter))

    def attend(tick):
        rid = lax.broadcasted_iota(jnp.int32, (TOK, TOK), 0)
        cid = lax.broadcasted_iota(jnp.int32, (TOK, TOK), 1)

        def upright(row):
            return jnp.sum(jnp.where(rid == cid, jnp.broadcast_to(row, (TOK, TOK)), 0.0), axis=1, keepdims=True)

        back = upright((pos if tick == 0 else pbuf)[...].astype(F32))
        seen = (cid <= rid) & (cid.astype(F32) >= rid.astype(F32) - back)
        loop(NZ - 1 + tick, lambda n: a2a_recv(tick, NZ - 2 + tick - n).wait_recv())
        v = arb[tick].astype(F32).reshape(NZ, 2, ROWS, HEAD)
        if tick:
            loop(2 * NZ, lambda m: remote(ssb, srb.at[m], sqs.at[m], sqr.at[m], sib).wait_recv())
            scale = upright(lax.rsqrt(jnp.sum(srb[...], axis=0) / (4.0 * HALF) + 1e-05))
        for h in range(2):
            keys = v[:, h].reshape(TOK, HEAD)
            if tick:
                keys = (keys * scale).astype(BF16).astype(F32)
            qg = qgain[:, pl.ds(pl.multiple_of(tp * TILE + h * HEAD, HEAD), HEAD)]
            query = (keys * qg).astype(BF16)
            keys = keys.astype(BF16)
            scores = lax.dot_general(query, keys, (((1,), (1,)), ((), ())), preferred_element_type=F32) * HEAD ** (-0.5)
            scores = jnp.where(seen, scores, -1e30)
            top = jnp.max(scores, axis=1, keepdims=True)
            expo = jnp.where(seen, jnp.exp(scores - top), 0.0)
            weights = (expo / jnp.sum(expo, axis=1, keepdims=True)).astype(BF16)
            cbuf[tick, 0, :, h * HEAD : (h + 1) * HEAD] = dot(weights, keys).astype(BF16)

    def swap_context(tick):
        return remote(cbuf.at[tick, 0], cbuf.at[tick, 1], css.at[tick], crs.at[tick], sib)

    def part_terms(tick, j):
        n = PART // TILE
        for g in range(2):
            if g == 1 and j == 0:
                swap_context(tick).wait_recv()
            for h in range(2):
                for i in range(n):
                    place = (slice(None), slice(h * 8, h * 8 + 8), slice(j * PART + i * TILE, j * PART + (i + 1) * TILE))
                    rotated = dot(cbuf[tick, g], wb[g, h * 8 + j * n + i])
                    bound = dot(jnp.abs(rotated).astype(BF16), means[...]) * LIMIT + LIMIT * 1e-06
                    term = jnp.clip(rotated, -bound, bound).reshape(NZ, ROWS, TILE)
                    terms[place] = term if g == 0 else terms[place] + term

    def chain(tick, dist, d, j):
        hops = dist if dist == NEAR + 1 else 1
        to = (sec, far(hops if d == 0 else NZ - hops) * 2 + k)
        cols = pl.ds(j * PART, PART)
        return remote(
            sb.at[tick, dist - 1, d, :, cols], rb.at[tick, dist - 1, d, :, cols],
            rss.at[tick, dist - 1, d, j], rrs.at[tick, dist - 1, d, j], to,
        )

    def step(tick, dist, d, j):
        if dist == 8 and j % 2 != d:
            return
        cols = slice(j * PART, (j + 1) * PART)
        v = terms[far(dist if d == 0 else NZ - dist), :, cols]
        if not (dist in (8, NEAR) or (dist == 7 and j % 2 != d)):
            chain(tick, dist + 1, d, j).wait_recv()
            v = v + rb[tick, dist, d, :, cols].astype(F32)
        sb[tick, dist - 1, d, :, cols] = v.astype(BF16)
        chain(tick, dist, d, j).start()

    def chain_sent(tick):
        def one(q):
            for j in range(NSUB):
                cols = pl.ds(j * PART, PART)
                src = sb.at[tick, q // 2, lax.rem(q, 2), :, cols]
                remote(
                    src, rb.at[tick, q // 2, lax.rem(q, 2), :, cols],
                    rss.at[tick, q // 2, lax.rem(q, 2), j], rrs.at[tick, q // 2, lax.rem(q, 2), j], sib,
                ).wait_send()

        loop(14, one)
        for j in range(NSUB):
            chain(tick, 8, j % 2, j).wait_send()

    def reduce(tick):
        for j in range(NSUB):
            part_terms(tick, j)
            for dist in (8, NEAR):
                for d in range(2):
                    step(tick, dist, d, j)
        for t in range(1, 8 - NEAR):
            for dist in (8 - t, NEAR - t):
                for j in range(NSUB):
                    for d in range(2):
                        step(tick, dist, d, j)

    def restore(tick):
        sums = []
        for j in range(NSUB):
            cols = slice(j * PART, (j + 1) * PART)
            summed = terms[z, :, cols]
            for dist in (1, NEAR + 1):
                for d in range(2):
                    chain(tick, dist, d, j).wait_recv()
                    summed = summed + rb[tick, dist - 1, d, :, cols].astype(F32)
            sums.append(summed)
        summed = jnp.concatenate(sums, axis=1)
        n = HALF // BLOCK
        tall = jnp.concatenate([summed[:, b * BLOCK : (b + 1) * BLOCK] for b in range(n)], axis=0)
        rescale = jnp.mean(jnp.abs(tall), axis=1, keepdims=True) + 1e-06
        recoded = jnp.clip(tall / rescale, -LIMIT, LIMIT).astype(BF16)
        back = dot(recoded, signs[0:BLOCK, 0:BLOCK]) * (rescale / BLOCK)
        wide = jnp.concatenate([back[b * 16 : (b + 1) * 16] for b in range(n)], axis=1)
        return (st[...] + wide).astype(BF16)

    def final(c, j):
        cols = pl.ds(j * TILE, TILE)
        return remote(
            fsb.at[c, :, cols], frb.at[k, :, cols], fss.at[c, j], frs.at[k, j], (nxt, z * 2 + c)
        )

    attend(0)
    swap_context(0).start()
    reduce(0)
    gains.wait_recv()
    rows = restore(0)
    rsb[...] = rows
    wide = rows.astype(F32)
    squares = jnp.sum(wide * wide, axis=1, keepdims=True)
    token = lax.broadcasted_iota(jnp.int32, (ROWS, TOK), 0) + z * ROWS
    lane = lax.broadcasted_iota(jnp.int32, (ROWS, TOK), 1)
    ssb[...] = jnp.sum(jnp.where(token == lane, squares[0:8] + squares[8:16], 0.0), axis=0, keepdims=True)
    loop(NZ, lambda n: (square_copy(n, 0).start(), square_copy(n, 1).start()))
    for jj in range(NZ):
        h, c = jj // 8, (jj % 8) * TILE
        message(1, jj, wide[8 * h : 8 * h + 8, c : c + TILE] * gbuf[:, wcols(jj, k)])
    loop(NZ, lambda n: a2a_copy(1, farthest(n)).start())
    residual = remote(rsb, rrb, mss.at[4], mrs.at[4], (nxt, z * 2 + k))
    residual.start()

    for c in packs + [gains, places]:
        c.wait_send()
    loop(NZ, lambda jj: wremote(jj).wait_send())
    loop(NZ - 1, lambda n: a2a_copy(0, farthest(n)).wait_send())
    for i in relayed:
        pl.when(passes(i))(lambda i=i: pass_copy(i).wait_send())
    swap_context(0).wait_send()
    chain_sent(0)
    places.wait_recv()

    attend(1)
    swap_context(1).start()
    reduce(1)
    residual.wait_recv()
    st[...] = rrb[...].astype(F32)
    rows = restore(1).astype(F32)
    for j in range(NSUB):
        v = rows[:, j * PART : (j + 1) * PART]
        pair = [swap(v[8 * h : 8 * h + 8, 0:TILE], v[8 * h : 8 * h + 8, TILE:PART]) for h in range(2)]
        for c in range(2):
            fsb[c, :, j * TILE : (j + 1) * TILE] = jnp.concatenate([pair[0][c], pair[1][c]], axis=0).astype(BF16)
    for j in range(NSUB):
        for c in range(2):
            final(c, j).start()

    residual.wait_send()
    loop(NZ, lambda n: (a2a_copy(1, n).wait_send(), square_copy(n, 0).wait_send(), square_copy(n, 1).wait_send()))
    swap_context(1).wait_send()
    chain_sent(1)
    for c in range(2):
        for j in range(NSUB):
            cols = pl.ds(j * TILE, TILE)
            remote(
                fsb.at[c, :, cols], frb.at[c, :, cols], fss.at[c, j], frs.at[c, j], (nxt, z * 2 + c)
            ).wait_recv()
    got = [frb[c].astype(F32) for c in range(2)]
    pieces = []
    for jj in range(NZ):
        h, j = jj // 8, (jj % 8) // 2
        for c in range(2):
            v = got[c][8 * h : 8 * h + 8, j * TILE : (j + 1) * TILE]
            pieces.append(pltpu.roll(v, 4, 0) if jj % 2 else v)
    out[0] = jnp.concatenate(pieces, axis=1)[0:4].astype(BF16)
    for c in range(2):
        for j in range(NSUB):
            final(c, j).wait_send()


def per_device(hidden, norm_gain, q_gain, out_weight, positions):
    vmem = pl.BlockSpec(memory_space=pltpu.VMEM)
    dma = pltpu.SemaphoreType.DMA
    return pl.pallas_call(
        kernel,
        out_shape=jax.ShapeDtypeStruct(hidden.shape, BF16),
        in_specs=[pl.BlockSpec(memory_space=pltpu.HBM)] * 5,
        out_specs=vmem,
        scratch_shapes=[
            pltpu.VMEM((1, 4, 8192), BF16),
            pltpu.VMEM((1, 8192), F32),
            pltpu.VMEM((1, 8192), F32),
            pltpu.VMEM((1, TOK), jnp.int32),
            pltpu.VMEM((TILE, TILE), BF16),
            pltpu.VMEM((TILE, TILE), BF16),
            pltpu.VMEM((8, 8192), F32),
            pltpu.VMEM((16, HALF), F32),
            pltpu.VMEM((2, NZ, TILE, TILE), BF16),
            pltpu.VMEM((4, 16, 1024), BF16),
            pltpu.VMEM((2, 16, 1024), BF16),
            pltpu.VMEM((1, 8192), F32),
            pltpu.VMEM((1, TOK), jnp.int32),
            pltpu.VMEM((2, NZ, 16, HEAD), BF16),
            pltpu.VMEM((2, NZ, 16, HEAD), BF16),
            pltpu.VMEM((2, 2, TOK, TILE), BF16),
            pltpu.VMEM((NZ, 16, HALF), F32),
            pltpu.VMEM((2, 8, 2, 16, HALF), BF16),
            pltpu.VMEM((2, 8, 2, 16, HALF), BF16),
            pltpu.VMEM((1, TOK), F32),
            pltpu.VMEM((2 * NZ, 1, TOK), F32),
            pltpu.VMEM((16, HALF), BF16),
            pltpu.VMEM((16, HALF), BF16),
            pltpu.VMEM((2, 16, 1024), BF16),
            pltpu.VMEM((2, 16, 1024), BF16),
            pltpu.VMEM((7, 16, HEAD), BF16),
            dma((4,)),
            dma((NZ,)),
            dma((NZ,)),
            dma((NZ,)),
            dma((5,)),
            dma((5,)),
            dma((2, NZ)),
            dma((2, NZ)),
            dma((2,)),
            dma((2,)),
            dma((2, 8, 2, NSUB)),
            dma((2, 8, 2, NSUB)),
            dma((2, NSUB)),
            dma((2, NSUB)),
            dma((7,)),
            dma((7,)),
            dma((2 * NZ,)),
            dma((2 * NZ,)),
        ],
        compiler_params=pltpu.CompilerParams(
            collective_id=0, has_side_effects=True, vmem_limit_bytes=60 * 1024 * 1024
        ),
    )(hidden, norm_gain, q_gain, out_weight, positions)


def solution(mesh):
    return jax.shard_map(
        per_device,
        mesh=mesh,
        in_specs=(
            P("section", "tp", None),
            P("section", None),
            P("section", None),
            P("section", "tp", None),
            P("section", None),
        ),
        out_specs=P("section", "tp", None),
        check_vma=False,
    )
```

```python
import jax
import jax.numpy as jnp
from jax import lax
from jax.experimental import pallas as pl
from jax.experimental.pallas import tpu as pltpu
from jax.sharding import PartitionSpec as P

MESH = pl.DeviceIdType.MESH
F32 = jnp.float32
BF16 = jnp.bfloat16
HEAD = 128
BLOCK = 128
TICKS = 2
LIMIT = 3.0
NZ = 16
TILE = 256
TOK = 128
ROWS = 8
HALF = 2048
NSUB = 4
PART = HALF // NSUB
AHEAD = 3
EARLY = 6
NEAR = 4


def constants():
    rows = lax.broadcasted_iota(jnp.int32, (TILE, TILE), 0)
    cols = lax.broadcasted_iota(jnp.int32, (TILE, TILE), 1)
    same = jnp.right_shift(rows, 7) == jnp.right_shift(cols, 7)
    both = jnp.bitwise_and(rows, cols)
    for shift in (4, 2, 1):
        both = jnp.bitwise_xor(both, jnp.right_shift(both, shift)) if shift != 4 else jnp.bitwise_xor(
            jnp.bitwise_and(both, 15), jnp.bitwise_and(jnp.right_shift(both, 4), 7)
        )
    sign = (1 - 2 * jnp.bitwise_and(both, 1)).astype(F32)
    signs = jnp.where(same, sign, 0.0).astype(BF16)
    means = jnp.where(same, 1.0 / BLOCK, 0.0).astype(BF16)
    return signs, means


def swap(p, q):
    low = lax.broadcasted_iota(jnp.int32, p.shape, 0) < 4
    return (
        jnp.where(low, p, pltpu.roll(q, 4, 0)),
        jnp.where(low, pltpu.roll(p, 4, 0), q),
    )


def dot(a, b):
    return jnp.dot(a, b, preferred_element_type=F32)


def kernel(
    hidden_hbm, gain_hbm, qgain_hbm, weight, pos_hbm, out,
    hidden, gain, qgain, pos,
    signs, means, x8, st, wb, msb, mrb, gbuf, pbuf, asb, arb, cbuf, terms, sb, rb, ssb, srb, rsb, rrb, fsb, frb, rly,
    lsem, wsem, wss, wrs, mss, mrs, ass, ars, css, crs, rss, rrs, fss, frs, pss, rlr, sqs, sqr,
):
    sec = lax.axis_index("section")
    tp = lax.axis_index("tp")
    nsec = lax.axis_size("section")
    z = tp // 2
    k = lax.rem(tp, 2)
    sib = (sec, z * 2 + 1 - k)
    nxt = lax.rem(sec + 1, nsec)
    prv = lax.rem(sec + nsec - 1, nsec)

    def far(i):
        return lax.rem(z + i, NZ)

    def farthest(n):
        half = (n + 1) // 2
        return far(NZ // 2 + half * (1 - 2 * lax.rem(n, 2)) + NZ)

    def remote(src, dst, send, recv, device):
        return pltpu.make_async_remote_copy(
            src_ref=src, dst_ref=dst, send_sem=send, recv_sem=recv, device_id=device, device_id_type=MESH
        )

    def wcols(jj, parity):
        return pl.ds(pl.multiple_of((2 * jj + parity) * TILE, TILE), TILE)

    def wlocal(jj):
        return pltpu.make_async_copy(weight.at[0, :, wcols(jj, k)], wb.at[0, jj], wsem.at[jj // 4])

    def wremote(jj):
        return remote(weight.at[0, :, wcols(jj, 1 - k)], wb.at[1, jj], wss.at[0], wrs.at[jj // 4], sib)

    def loop(n, body):
        lax.fori_loop(0, n, lambda i, c: (body(i), c)[1], 0)

    loads = [
        pltpu.make_async_copy(src, dst, lsem.at[i])
        for i, (src, dst) in enumerate(
            ((hidden_hbm, hidden), (gain_hbm, gain), (pos_hbm, pos), (qgain_hbm, qgain))
        )
    ]
    for c in loads[:2]:
        c.start()

    barrier = pltpu.get_barrier_semaphore()

    def greet(section, member):
        pl.semaphore_signal(barrier, inc=1, device_id=(section, member), device_id_type=MESH)

    order = [8, 7, 9, 6, 10, 5, 11, 4, 12, 3, 13, 2, 14, 1, 15]
    relayed = [i for i in order if 4 < i < 12]

    def by_relay(source, i):
        return jnp.logical_and(source < EARLY, lax.rem(source + i, NZ) >= EARLY)

    for i in order:
        if i in relayed:
            pl.when(jnp.logical_not(by_relay(far(NZ - i), i)))(lambda i=i: greet(sec, far(NZ - i) * 2 + k))
        else:
            greet(sec, far(NZ - i) * 2 + k)
    greet(*sib)
    greet(prv, z * 2 + k)
    greet(prv, z * 2 + 1 - k)
    greet(nxt, z * 2 + k)
    direct = NZ - 1 + 4
    for i in relayed:
        direct = direct - by_relay(z, i).astype(jnp.int32)

    for c in loads[2:]:
        c.start()
    loop(NZ, lambda jj: wlocal(jj).start())

    loads[0].wait()
    x = hidden[0].astype(F32)
    x8[0:4, :] = x
    x8[4:8, :] = x
    x = x8[...]
    scale = lax.rsqrt(jnp.mean(x * x, axis=1, keepdims=True) + 1e-05)
    loads[1].wait()
    normed = x * scale * gain[...]

    def pack(v, parity):
        quarters = []
        for q in range(4):
            quarters.append(
                jnp.concatenate(
                    [v[:, (2 * jj + parity) * TILE : (2 * jj + parity + 1) * TILE] for jj in range(4 * q, 4 * q + 4)],
                    axis=1,
                )
            )
        return jnp.concatenate([swap(quarters[0], quarters[1])[0], swap(quarters[2], quarters[3])[0]], axis=0)

    even = k == 0

    def pack_both(i, v):
        p0, p1 = pack(v, 0), pack(v, 1)
        msb[i] = jnp.where(even, p0, p1).astype(BF16)
        msb[2 + i] = jnp.where(even, p1, p0).astype(BF16)

    pack_both(0, normed)
    pl.semaphore_wait(barrier, direct)
    packs = [remote(msb.at[2 + i], mrb.at[i], mss.at[i], mrs.at[i], sib) for i in range(2)]
    packs[0].start()
    pack_both(1, x)
    gains = remote(gain, gbuf, mss.at[2], mrs.at[2], (prv, z * 2 + k))
    places = remote(pos, pbuf, mss.at[3], mrs.at[3], (nxt, z * 2 + k))

    def unpack(i):
        mine, other = msb[i].astype(F32), mrb[i].astype(F32)
        a = jnp.where(even, mine, other)
        b = jnp.where(even, other, mine)
        halves = [jnp.concatenate(swap(a[8 * h : 8 * h + 8], b[8 * h : 8 * h + 8]), axis=1) for h in range(2)]
        return jnp.concatenate(halves, axis=0)

    def a2a_copy(tick, j):
        return remote(
            asb.at[tick, j], arb.at[tick, z], ass.at[tick], ars.at[tick], (sec if tick == 0 else nxt, j * 2 + k)
        )

    def a2a_all(tick):
        some = pl.ds(0, NZ - 1 + tick)
        return remote(asb.at[tick, some], arb.at[tick, some], ass.at[tick], ars.at[tick], sib)

    def message(tick, jj, v):
        asb[tick, jj] = jnp.concatenate([v[:, 0:HEAD], v[:, HEAD:TILE]], axis=0).astype(BF16)

    def square_copy(n, c):
        j = farthest(n)
        return remote(ssb.at[j * 2 + c], srb.at[tp], sqs.at[0], sqr.at[0], (nxt, j * 2 + c))

    def squares_all():
        return remote(ssb, srb, sqs.at[0], sqr.at[0], sib)

    def pass_copy(i):
        origin = far(NZ - 4 if i <= 8 else 4)
        to = (sec, lax.rem(origin + i, NZ) * 2 + k)
        return remote(rly.at[i - 5], arb.at[0, origin], pss.at[i - 5], ars.at[0], to)

    def relay_copy(i):
        to = (sec, far(4 if i <= 8 else NZ - 4) * 2 + k)
        return remote(asb.at[0, far(i)], rly.at[i - 5], ass.at[0], rlr.at[i - 5], to)

    def passes(i):
        return by_relay(far(NZ - 4 if i <= 8 else 4), i)

    def first_sends():
        for i in order:
            if i in relayed:
                pl.when(by_relay(z, i))(lambda i=i: relay_copy(i).start())
                pl.when(jnp.logical_not(by_relay(z, i)))(lambda i=i: a2a_copy(0, far(i)).start())
            else:
                a2a_copy(0, far(i)).start()
        arb[0, z] = asb[0, z]

        packs[1].start()
        loop(NZ, lambda jj: wremote(jj).start())
        loads[2].wait()
        loads[3].wait()
        gains.start()
        places.start()

        def hand_on(i):
            relay_copy(i).wait_recv()
            pass_copy(i).start()

        for i in relayed:
            pl.when(passes(i))(lambda i=i: hand_on(i))

    packs[0].wait_recv()
    rows = unpack(0)
    for jj in range(NZ):
        h, c = jj // 8, (jj % 8) * TILE
        message(0, jj, rows[8 * h : 8 * h + 8, c : c + TILE])
    first_sends()
    packs[1].wait_recv()
    st[...] = unpack(1)

    def rotate(g, quarter):
        places = [quarter * 4 + i for i in range(4)]
        four = wb.at[g, pl.ds(quarter * 4, 4)]
        if g == 0:
            pltpu.make_async_copy(four, four, wsem.at[quarter]).wait()
        else:
            remote(four, four, wss.at[0], wrs.at[quarter], sib).wait_recv()
        for jj in places:
            wb[g, jj] = dot(wb[g, jj], signs[...]).astype(BF16)

    sg, mn = constants()
    signs[...] = sg
    means[...] = mn
    loop(4, lambda quarter: rotate(0, quarter))
    loop(4, lambda quarter: rotate(1, quarter))

    def attend(tick):
        rid = lax.broadcasted_iota(jnp.int32, (TOK, TOK), 0)
        cid = lax.broadcasted_iota(jnp.int32, (TOK, TOK), 1)

        def upright(row):
            return jnp.sum(jnp.where(rid == cid, jnp.broadcast_to(row, (TOK, TOK)), 0.0), axis=1, keepdims=True)

        back = upright((pos if tick == 0 else pbuf)[...].astype(F32))
        seen = (cid <= rid) & (cid.astype(F32) >= rid.astype(F32) - back)
        a2a_all(tick).wait_recv()
        v = arb[tick].astype(F32).reshape(NZ, 2, ROWS, HEAD)
        if tick:
            squares_all().wait_recv()
            scale = upright(lax.rsqrt(jnp.sum(srb[...], axis=0) / (4.0 * HALF) + 1e-05))
        for h in range(2):
            keys = v[:, h].reshape(TOK, HEAD)
            if tick:
                keys = (keys * scale).astype(BF16).astype(F32)
            qg = qgain[:, pl.ds(pl.multiple_of(tp * TILE + h * HEAD, HEAD), HEAD)]
            query = (keys * qg).astype(BF16)
            keys = keys.astype(BF16)
            scores = lax.dot_general(query, keys, (((1,), (1,)), ((), ())), preferred_element_type=F32) * HEAD ** (-0.5)
            scores = jnp.where(seen, scores, -1e30)
            top = jnp.max(scores, axis=1, keepdims=True)
            expo = jnp.where(seen, jnp.exp(scores - top), 0.0)
            weights = (expo / jnp.sum(expo, axis=1, keepdims=True)).astype(BF16)
            cbuf[tick, 0, :, h * HEAD : (h + 1) * HEAD] = dot(weights, keys).astype(BF16)

    def swap_context(tick):
        return remote(cbuf.at[tick, 0], cbuf.at[tick, 1], css.at[tick], crs.at[tick], sib)

    def part_terms(tick, g, j):
        n = PART // TILE
        for h in range(2):
            for i in range(n):
                place = (slice(None), slice(h * 8, h * 8 + 8), slice(j * PART + i * TILE, j * PART + (i + 1) * TILE))
                rotated = dot(cbuf[tick, g], wb[g, h * 8 + j * n + i])
                bound = dot(jnp.abs(rotated).astype(BF16), means[...]) * LIMIT + LIMIT * 1e-06
                term = jnp.clip(rotated, -bound, bound).reshape(NZ, ROWS, TILE)
                terms[place] = term if g == 0 else terms[place] + term

    def chain(tick, dist, d, j):
        hops = dist if dist == NEAR + 1 else 1
        to = (sec, far(hops if d == 0 else NZ - hops) * 2 + k)
        cols = pl.ds(j * PART, PART)
        return remote(
            sb.at[tick, dist - 1, d, :, cols], rb.at[tick, dist - 1, d, :, cols],
            rss.at[tick, dist // 8], rrs.at[tick, dist - 1, d, j // 2], to,
        )

    def arrive(tick, dist, d, j):
        if dist == 8:
            chain(tick, 8, d, j).wait_recv()
        elif j % 2 == 0:
            both = rb.at[tick, dist - 1, d, :, pl.ds(j * PART, 2 * PART)]
            remote(both, both, rss.at[tick, 0], rrs.at[tick, dist - 1, d, j // 2], sib).wait_recv()

    def step(tick, dist, d, j):
        if dist == 8 and j % 2 != d:
            return
        cols = slice(j * PART, (j + 1) * PART)
        v = terms[far(dist if d == 0 else NZ - dist), :, cols]
        if not (dist in (8, NEAR) or (dist == 7 and j % 2 != d)):
            arrive(tick, dist + 1, d, j)
            v = v + rb[tick, dist, d, :, cols].astype(F32)
        sb[tick, dist - 1, d, :, cols] = v.astype(BF16)
        chain(tick, dist, d, j).start()

    def chain_sent(tick):
        most, rest = sb.at[tick, pl.ds(0, 7)], sb.at[tick, 7, 0]
        remote(most, most, rss.at[tick, 0], rrs.at[tick, 0, 0, 0], sib).wait_send()
        remote(rest, rest, rss.at[tick, 1], rrs.at[tick, 0, 0, 0], sib).wait_send()

    def reduce(tick):
        for j in range(AHEAD):
            part_terms(tick, 0, j)
        swap_context(tick).wait_recv()
        for j in range(NSUB):
            if j >= AHEAD:
                part_terms(tick, 0, j)
            part_terms(tick, 1, j)
            for dist in (8, NEAR):
                for d in range(2):
                    step(tick, dist, d, j)
        for t in range(1, 8 - NEAR):
            for dist in (8 - t, NEAR - t):
                for j in range(NSUB):
                    for d in range(2):
                        step(tick, dist, d, j)

    def restore(tick):
        sums = []
        for j in range(NSUB):
            cols = slice(j * PART, (j + 1) * PART)
            summed = terms[z, :, cols]
            for dist in (1, NEAR + 1):
                for d in range(2):
                    arrive(tick, dist, d, j)
                    summed = summed + rb[tick, dist - 1, d, :, cols].astype(F32)
            sums.append(summed)
        summed = jnp.concatenate(sums, axis=1)
        n = HALF // BLOCK
        tall = jnp.concatenate([summed[:, b * BLOCK : (b + 1) * BLOCK] for b in range(n)], axis=0)
        rescale = jnp.mean(jnp.abs(tall), axis=1, keepdims=True) + 1e-06
        recoded = jnp.clip(tall / rescale, -LIMIT, LIMIT).astype(BF16)
        back = dot(recoded, signs[0:BLOCK, 0:BLOCK]) * (rescale / BLOCK)
        wide = jnp.concatenate([back[b * 16 : (b + 1) * 16] for b in range(n)], axis=1)
        return (st[...] + wide).astype(BF16)

    def final(c, j):
        cols = pl.ds(j * TILE, TILE)
        return remote(fsb.at[c, :, cols], frb.at[k, :, cols], fss.at[0], frs.at[0], (nxt, z * 2 + c))

    finals = remote(fsb, frb, fss.at[0], frs.at[0], sib)

    attend(0)
    swap_context(0).start()
    reduce(0)
    gains.wait_recv()
    rows = restore(0)
    rsb[...] = rows
    wide = rows.astype(F32)
    squares = jnp.sum(wide * wide, axis=1, keepdims=True)
    token = lax.broadcasted_iota(jnp.int32, (ROWS, TOK), 0) + z * ROWS
    lane = lax.broadcasted_iota(jnp.int32, (ROWS, TOK), 1)
    squares = jnp.sum(jnp.where(token == lane, squares[0:8] + squares[8:16], 0.0), axis=0, keepdims=True)
    for m in range(2 * NZ):
        ssb[m] = squares
    loop(NZ, lambda n: (square_copy(n, 0).start(), square_copy(n, 1).start()))
    for jj in range(NZ):
        h, c = jj // 8, (jj % 8) * TILE
        message(1, jj, wide[8 * h : 8 * h + 8, c : c + TILE] * gbuf[:, wcols(jj, k)])
    loop(NZ, lambda n: a2a_copy(1, farthest(n)).start())
    residual = remote(rsb, rrb, mss.at[4], mrs.at[4], (nxt, z * 2 + k))
    residual.start()

    for c in packs + [gains, places]:
        c.wait_send()
    remote(wb.at[1], wb.at[1], wss.at[0], wrs.at[0], sib).wait_send()
    a2a_all(0).wait_send()
    for i in relayed:
        pl.when(passes(i))(lambda i=i: pass_copy(i).wait_send())
    swap_context(0).wait_send()
    chain_sent(0)
    places.wait_recv()

    attend(1)
    swap_context(1).start()
    reduce(1)
    residual.wait_recv()
    st[...] = rrb[...].astype(F32)
    rows = restore(1).astype(F32)
    for j in range(NSUB):
        v = rows[:, j * PART : (j + 1) * PART]
        pair = [swap(v[8 * h : 8 * h + 8, 0:TILE], v[8 * h : 8 * h + 8, TILE:PART]) for h in range(2)]
        for c in range(2):
            fsb[c, :, j * TILE : (j + 1) * TILE] = jnp.concatenate([pair[0][c], pair[1][c]], axis=0).astype(BF16)
    for j in range(NSUB):
        for c in range(2):
            final(c, j).start()

    residual.wait_send()
    a2a_all(1).wait_send()
    squares_all().wait_send()
    swap_context(1).wait_send()
    chain_sent(1)
    finals.wait_recv()
    got = [frb[c].astype(F32) for c in range(2)]
    pieces = []
    for jj in range(NZ):
        h, j = jj // 8, (jj % 8) // 2
        for c in range(2):
            v = got[c][8 * h : 8 * h + 8, j * TILE : (j + 1) * TILE]
            pieces.append(pltpu.roll(v, 4, 0) if jj % 2 else v)
    out[0] = jnp.concatenate(pieces, axis=1)[0:4].astype(BF16)
    finals.wait_send()


def per_device(hidden, norm_gain, q_gain, out_weight, positions):
    vmem = pl.BlockSpec(memory_space=pltpu.VMEM)
    dma = pltpu.SemaphoreType.DMA
    return pl.pallas_call(
        kernel,
        out_shape=jax.ShapeDtypeStruct(hidden.shape, BF16),
        in_specs=[pl.BlockSpec(memory_space=pltpu.HBM)] * 5,
        out_specs=vmem,
        scratch_shapes=[
            pltpu.VMEM((1, 4, 8192), BF16),
            pltpu.VMEM((1, 8192), F32),
            pltpu.VMEM((1, 8192), F32),
            pltpu.VMEM((1, TOK), jnp.int32),
            pltpu.VMEM((TILE, TILE), BF16),
            pltpu.VMEM((TILE, TILE), BF16),
            pltpu.VMEM((8, 8192), F32),
            pltpu.VMEM((16, HALF), F32),
            pltpu.VMEM((2, NZ, TILE, TILE), BF16),
            pltpu.VMEM((4, 16, 1024), BF16),
            pltpu.VMEM((2, 16, 1024), BF16),
            pltpu.VMEM((1, 8192), F32),
            pltpu.VMEM((1, TOK), jnp.int32),
            pltpu.VMEM((2, NZ, 16, HEAD), BF16),
            pltpu.VMEM((2, NZ, 16, HEAD), BF16),
            pltpu.VMEM((2, 2, TOK, TILE), BF16),
            pltpu.VMEM((NZ, 16, HALF), F32),
            pltpu.VMEM((2, 8, 2, 16, HALF), BF16),
            pltpu.VMEM((2, 8, 2, 16, HALF), BF16),
            pltpu.VMEM((2 * NZ, 1, TOK), F32),
            pltpu.VMEM((2 * NZ, 1, TOK), F32),
            pltpu.VMEM((16, HALF), BF16),
            pltpu.VMEM((16, HALF), BF16),
            pltpu.VMEM((2, 16, 1024), BF16),
            pltpu.VMEM((2, 16, 1024), BF16),
            pltpu.VMEM((7, 16, HEAD), BF16),
            dma((4,)),
            dma((4,)),
            dma((1,)),
            dma((4,)),
            dma((5,)),
            dma((5,)),
            dma((2,)),
            dma((2,)),
            dma((2,)),
            dma((2,)),
            dma((2, 2)),
            dma((2, 8, 2, 2)),
            dma((1,)),
            dma((1,)),
            dma((7,)),
            dma((7,)),
            dma((1,)),
            dma((1,)),
        ],
        compiler_params=pltpu.CompilerParams(
            collective_id=0, has_side_effects=True, vmem_limit_bytes=60 * 1024 * 1024
        ),
    )(hidden, norm_gain, q_gain, out_weight, positions)


def solution(mesh):
    return jax.shard_map(
        per_device,
        mesh=mesh,
        in_specs=(
            P("section", "tp", None),
            P("section", None),
            P("section", None),
            P("section", "tp", None),
            P("section", None),
        ),
        out_specs=P("section", "tp", None),
        check_vma=False,
    )
```

```python
import jax
import jax.numpy as jnp
from jax import lax
from jax.experimental import pallas as pl
from jax.experimental.pallas import tpu as pltpu
from jax.sharding import PartitionSpec as P

MESH = pl.DeviceIdType.MESH
F32 = jnp.float32
BF16 = jnp.bfloat16
HEAD = 128
BLOCK = 128
TICKS = 2
LIMIT = 3.0
NZ = 16
TILE = 256
TOK = 128
ROWS = 8
HALF = 2048
NSUB = 4
PART = HALF // NSUB
AHEAD = 3
EARLY = 4
NEAR = 4


def constants():
    rows = lax.broadcasted_iota(jnp.int32, (TILE, TILE), 0)
    cols = lax.broadcasted_iota(jnp.int32, (TILE, TILE), 1)
    same = jnp.right_shift(rows, 7) == jnp.right_shift(cols, 7)
    both = jnp.bitwise_and(rows, cols)
    for shift in (4, 2, 1):
        both = jnp.bitwise_xor(both, jnp.right_shift(both, shift)) if shift != 4 else jnp.bitwise_xor(
            jnp.bitwise_and(both, 15), jnp.bitwise_and(jnp.right_shift(both, 4), 7)
        )
    sign = (1 - 2 * jnp.bitwise_and(both, 1)).astype(F32)
    signs = jnp.where(same, sign, 0.0).astype(BF16)
    means = jnp.where(same, 1.0 / BLOCK, 0.0).astype(BF16)
    return signs, means


def swap(p, q):
    low = lax.broadcasted_iota(jnp.int32, p.shape, 0) < 4
    return (
        jnp.where(low, p, pltpu.roll(q, 4, 0)),
        jnp.where(low, pltpu.roll(p, 4, 0), q),
    )


def dot(a, b):
    return jnp.dot(a, b, preferred_element_type=F32)


def kernel(
    hidden_hbm, gain_hbm, qgain_hbm, weight, pos_hbm, out,
    hidden, gain, qgain, pos,
    signs, means, x8, st, wb, msb, mrb, gbuf, pbuf, asb, arb, cbuf, terms, sb, rb, ssb, srb, rsb, rrb, fsb, frb, rly,
    lsem, wsem, wss, wrs, mss, mrs, ass, ars, css, crs, rss, rrs, fss, frs, pss, rlr, sqs, sqr,
):
    sec = lax.axis_index("section")
    tp = lax.axis_index("tp")
    nsec = lax.axis_size("section")
    z = tp // 2
    k = lax.rem(tp, 2)
    sib = (sec, z * 2 + 1 - k)
    nxt = lax.rem(sec + 1, nsec)
    prv = lax.rem(sec + nsec - 1, nsec)

    def far(i):
        return lax.rem(z + i, NZ)

    def farthest(n):
        half = (n + 1) // 2
        return far(NZ // 2 + half * (1 - 2 * lax.rem(n, 2)) + NZ)

    def remote(src, dst, send, recv, device):
        return pltpu.make_async_remote_copy(
            src_ref=src, dst_ref=dst, send_sem=send, recv_sem=recv, device_id=device, device_id_type=MESH
        )

    def wcols(jj, parity):
        return pl.ds(pl.multiple_of((2 * jj + parity) * TILE, TILE), TILE)

    def wlocal(jj):
        return pltpu.make_async_copy(weight.at[0, :, wcols(jj, k)], wb.at[0, jj], wsem.at[jj // 4])

    def wremote(jj):
        return remote(weight.at[0, :, wcols(jj, 1 - k)], wb.at[1, jj], wss.at[0], wrs.at[jj // 4], sib)

    def loop(n, body):
        lax.fori_loop(0, n, lambda i, c: (body(i), c)[1], 0)

    loads = [
        pltpu.make_async_copy(src, dst, lsem.at[i])
        for i, (src, dst) in enumerate(
            ((hidden_hbm, hidden), (gain_hbm, gain), (pos_hbm, pos), (qgain_hbm, qgain))
        )
    ]
    for c in loads[:2]:
        c.start()

    barrier = pltpu.get_barrier_semaphore()

    def greet(section, member):
        pl.semaphore_signal(barrier, inc=1, device_id=(section, member), device_id_type=MESH)

    order = [8, 7, 9, 6, 10, 5, 11, 4, 12, 3, 13, 2, 14, 1, 15]
    relayed = [i for i in order if 4 < i < 12]

    def by_relay(source, i):
        return jnp.logical_and(source < EARLY, lax.rem(source + i, NZ) >= EARLY)

    for i in order:
        if i in relayed:
            pl.when(jnp.logical_not(by_relay(far(NZ - i), i)))(lambda i=i: greet(sec, far(NZ - i) * 2 + k))
        else:
            greet(sec, far(NZ - i) * 2 + k)
    greet(*sib)
    greet(prv, z * 2 + k)
    greet(prv, z * 2 + 1 - k)
    greet(nxt, z * 2 + k)
    direct = NZ - 1 + 4
    for i in relayed:
        direct = direct - by_relay(z, i).astype(jnp.int32)

    for c in loads[2:]:
        c.start()
    loop(NZ, lambda jj: wlocal(jj).start())

    loads[0].wait()
    x = hidden[0].astype(F32)
    x8[0:4, :] = x
    x8[4:8, :] = x
    x = x8[...]
    scale = lax.rsqrt(jnp.mean(x * x, axis=1, keepdims=True) + 1e-05)
    loads[1].wait()
    normed = x * scale * gain[...]

    def pack(v, parity):
        quarters = []
        for q in range(4):
            quarters.append(
                jnp.concatenate(
                    [v[:, (2 * jj + parity) * TILE : (2 * jj + parity + 1) * TILE] for jj in range(4 * q, 4 * q + 4)],
                    axis=1,
                )
            )
        return jnp.concatenate([swap(quarters[0], quarters[1])[0], swap(quarters[2], quarters[3])[0]], axis=0)

    even = k == 0

    def pack_both(i, v):
        p0, p1 = pack(v, 0), pack(v, 1)
        msb[i] = jnp.where(even, p0, p1).astype(BF16)
        msb[2 + i] = jnp.where(even, p1, p0).astype(BF16)

    pack_both(0, normed)
    pl.semaphore_wait(barrier, direct)
    packs = [remote(msb.at[2 + i], mrb.at[i], mss.at[i], mrs.at[i], sib) for i in range(2)]
    packs[0].start()
    pack_both(1, x)
    gains = remote(gain, gbuf, mss.at[2], mrs.at[2], (prv, z * 2 + k))
    places = remote(pos, pbuf, mss.at[3], mrs.at[3], (nxt, z * 2 + k))

    def unpack(i):
        mine, other = msb[i].astype(F32), mrb[i].astype(F32)
        a = jnp.where(even, mine, other)
        b = jnp.where(even, other, mine)
        halves = [jnp.concatenate(swap(a[8 * h : 8 * h + 8], b[8 * h : 8 * h + 8]), axis=1) for h in range(2)]
        return jnp.concatenate(halves, axis=0)

    def a2a_copy(tick, j):
        return remote(
            asb.at[tick, j], arb.at[tick, z], ass.at[tick], ars.at[tick], (sec if tick == 0 else nxt, j * 2 + k)
        )

    def a2a_all(tick):
        some = pl.ds(0, NZ - 1 + tick)
        return remote(asb.at[tick, some], arb.at[tick, some], ass.at[tick], ars.at[tick], sib)

    def message(tick, jj, v):
        asb[tick, jj] = jnp.concatenate([v[:, 0:HEAD], v[:, HEAD:TILE]], axis=0).astype(BF16)

    def square_copy(n, c):
        j = farthest(n)
        return remote(ssb.at[j * 2 + c], srb.at[tp], sqs.at[0], sqr.at[0], (nxt, j * 2 + c))

    def squares_all():
        return remote(ssb, srb, sqs.at[0], sqr.at[0], sib)

    def pass_copy(i):
        origin = far(NZ - 4 if i <= 8 else 4)
        to = (sec, lax.rem(origin + i, NZ) * 2 + k)
        return remote(rly.at[i - 5], arb.at[0, origin], pss.at[i - 5], ars.at[0], to)

    def relay_copy(i):
        to = (sec, far(4 if i <= 8 else NZ - 4) * 2 + k)
        return remote(asb.at[0, far(i)], rly.at[i - 5], ass.at[0], rlr.at[i - 5], to)

    def passes(i):
        return by_relay(far(NZ - 4 if i <= 8 else 4), i)

    def first_sends():
        for i in order:
            if i in relayed:
                pl.when(by_relay(z, i))(lambda i=i: relay_copy(i).start())
                pl.when(jnp.logical_not(by_relay(z, i)))(lambda i=i: a2a_copy(0, far(i)).start())
            else:
                a2a_copy(0, far(i)).start()
        arb[0, z] = asb[0, z]

        packs[1].start()
        loop(NZ, lambda jj: wremote(jj).start())
        loads[2].wait()
        loads[3].wait()
        gains.start()
        places.start()

        def hand_on(i):
            relay_copy(i).wait_recv()
            pass_copy(i).start()

        for i in relayed:
            pl.when(passes(i))(lambda i=i: hand_on(i))

    packs[0].wait_recv()
    rows = unpack(0)
    for jj in range(NZ):
        h, c = jj // 8, (jj % 8) * TILE
        message(0, jj, rows[8 * h : 8 * h + 8, c : c + TILE])
    first_sends()
    packs[1].wait_recv()
    st[...] = unpack(1)

    def rotate(g, quarter):
        places = [quarter * 4 + i for i in range(4)]
        four = wb.at[g, pl.ds(quarter * 4, 4)]
        if g == 0:
            pltpu.make_async_copy(four, four, wsem.at[quarter]).wait()
        else:
            remote(four, four, wss.at[0], wrs.at[quarter], sib).wait_recv()
        for jj in places:
            wb[g, jj] = dot(wb[g, jj], signs[...]).astype(BF16)

    sg, mn = constants()
    signs[...] = sg
    means[...] = mn
    loop(4, lambda quarter: rotate(0, quarter))
    loop(4, lambda quarter: rotate(1, quarter))

    def attend(tick):
        rid = lax.broadcasted_iota(jnp.int32, (TOK, TOK), 0)
        cid = lax.broadcasted_iota(jnp.int32, (TOK, TOK), 1)

        def upright(row):
            return jnp.sum(jnp.where(rid == cid, jnp.broadcast_to(row, (TOK, TOK)), 0.0), axis=1, keepdims=True)

        back = upright((pos if tick == 0 else pbuf)[...].astype(F32))
        seen = (cid <= rid) & (cid.astype(F32) >= rid.astype(F32) - back)
        a2a_all(tick).wait_recv()
        v = arb[tick].astype(F32).reshape(NZ, 2, ROWS, HEAD)
        if tick:
            squares_all().wait_recv()
            scale = upright(lax.rsqrt(jnp.sum(srb[...], axis=0) / (4.0 * HALF) + 1e-05))
        for h in range(2):
            keys = v[:, h].reshape(TOK, HEAD)
            if tick:
                keys = (keys * scale).astype(BF16).astype(F32)
            qg = qgain[:, pl.ds(pl.multiple_of(tp * TILE + h * HEAD, HEAD), HEAD)]
            query = (keys * qg).astype(BF16)
            keys = keys.astype(BF16)
            scores = lax.dot_general(query, keys, (((1,), (1,)), ((), ())), preferred_element_type=F32) * HEAD ** (-0.5)
            scores = jnp.where(seen, scores, -1e30)
            top = jnp.max(scores, axis=1, keepdims=True)
            expo = jnp.where(seen, jnp.exp(scores - top), 0.0)
            weights = (expo / jnp.sum(expo, axis=1, keepdims=True)).astype(BF16)
            cbuf[tick, 0, :, h * HEAD : (h + 1) * HEAD] = dot(weights, keys).astype(BF16)

    def swap_context(tick):
        return remote(cbuf.at[tick, 0], cbuf.at[tick, 1], css.at[tick], crs.at[tick], sib)

    def part_terms(tick, g, j):
        n = PART // TILE
        for h in range(2):
            for i in range(n):
                place = (slice(None), slice(h * 8, h * 8 + 8), slice(j * PART + i * TILE, j * PART + (i + 1) * TILE))
                rotated = dot(cbuf[tick, g], wb[g, h * 8 + j * n + i])
                bound = dot(jnp.abs(rotated).astype(BF16), means[...]) * LIMIT + LIMIT * 1e-06
                term = jnp.clip(rotated, -bound, bound).reshape(NZ, ROWS, TILE)
                terms[place] = term if g == 0 else terms[place] + term

    def chain(tick, dist, d, j):
        hops = dist if dist == NEAR + 1 else 1
        to = (sec, far(hops if d == 0 else NZ - hops) * 2 + k)
        cols = pl.ds(j * PART, PART)
        return remote(
            sb.at[tick, dist - 1, d, :, cols], rb.at[tick, dist - 1, d, :, cols],
            rss.at[tick, dist // 8], rrs.at[tick, dist - 1, d, j // 2], to,
        )

    def arrive(tick, dist, d, j):
        if dist == 8:
            chain(tick, 8, d, j).wait_recv()
        elif j % 2 == 0:
            both = rb.at[tick, dist - 1, d, :, pl.ds(j * PART, 2 * PART)]
            remote(both, both, rss.at[tick, 0], rrs.at[tick, dist - 1, d, j // 2], sib).wait_recv()

    def step(tick, dist, d, j):
        if dist == 8 and j % 2 != d:
            return
        cols = slice(j * PART, (j + 1) * PART)
        v = terms[far(dist if d == 0 else NZ - dist), :, cols]
        if not (dist in (8, NEAR) or (dist == 7 and j % 2 != d)):
            arrive(tick, dist + 1, d, j)
            v = v + rb[tick, dist, d, :, cols].astype(F32)
        sb[tick, dist - 1, d, :, cols] = v.astype(BF16)
        chain(tick, dist, d, j).start()

    def chain_sent(tick):
        most, rest = sb.at[tick, pl.ds(0, 7)], sb.at[tick, 7, 0]
        remote(most, most, rss.at[tick, 0], rrs.at[tick, 0, 0, 0], sib).wait_send()
        remote(rest, rest, rss.at[tick, 1], rrs.at[tick, 0, 0, 0], sib).wait_send()

    def reduce(tick):
        for j in range(AHEAD):
            part_terms(tick, 0, j)
        swap_context(tick).wait_recv()
        for j in range(NSUB):
            if j >= AHEAD:
                part_terms(tick, 0, j)
            part_terms(tick, 1, j)
            for dist in (8, NEAR):
                for d in range(2):
                    step(tick, dist, d, j)
        for t in range(1, 8 - NEAR):
            for dist in (8 - t, NEAR - t):
                for j in range(NSUB):
                    for d in range(2):
                        step(tick, dist, d, j)

    def restore(tick):
        sums = []
        for j in range(NSUB):
            cols = slice(j * PART, (j + 1) * PART)
            summed = terms[z, :, cols]
            for dist in (1, NEAR + 1):
                for d in range(2):
                    arrive(tick, dist, d, j)
                    summed = summed + rb[tick, dist - 1, d, :, cols].astype(F32)
            sums.append(summed)
        summed = jnp.concatenate(sums, axis=1)
        n = HALF // BLOCK
        tall = jnp.concatenate([summed[:, b * BLOCK : (b + 1) * BLOCK] for b in range(n)], axis=0)
        rescale = jnp.mean(jnp.abs(tall), axis=1, keepdims=True) + 1e-06
        recoded = jnp.clip(tall / rescale, -LIMIT, LIMIT).astype(BF16)
        back = dot(recoded, signs[0:BLOCK, 0:BLOCK]) * (rescale / BLOCK)
        wide = jnp.concatenate([back[b * 16 : (b + 1) * 16] for b in range(n)], axis=1)
        return (st[...] + wide).astype(BF16)

    def final(c):
        return remote(fsb.at[c], frb.at[k], fss.at[0], frs.at[0], (nxt, z * 2 + c))

    finals = remote(fsb, frb, fss.at[0], frs.at[0], sib)

    attend(0)
    swap_context(0).start()
    reduce(0)
    gains.wait_recv()
    rows = restore(0)
    rsb[...] = rows
    wide = rows.astype(F32)
    squares = jnp.sum(wide * wide, axis=1, keepdims=True)
    token = lax.broadcasted_iota(jnp.int32, (ROWS, TOK), 0) + z * ROWS
    lane = lax.broadcasted_iota(jnp.int32, (ROWS, TOK), 1)
    squares = jnp.sum(jnp.where(token == lane, squares[0:8] + squares[8:16], 0.0), axis=0, keepdims=True)
    for m in range(2 * NZ):
        ssb[m] = squares
    loop(NZ, lambda n: (square_copy(n, 0).start(), square_copy(n, 1).start()))
    for jj in range(NZ):
        h, c = jj // 8, (jj % 8) * TILE
        message(1, jj, wide[8 * h : 8 * h + 8, c : c + TILE] * gbuf[:, wcols(jj, k)])
    loop(NZ, lambda n: a2a_copy(1, farthest(n)).start())
    residual = remote(rsb, rrb, mss.at[4], mrs.at[4], (nxt, z * 2 + k))
    residual.start()

    for c in packs + [gains, places]:
        c.wait_send()
    remote(wb.at[1], wb.at[1], wss.at[0], wrs.at[0], sib).wait_send()
    a2a_all(0).wait_send()
    for i in relayed:
        pl.when(passes(i))(lambda i=i: pass_copy(i).wait_send())
    swap_context(0).wait_send()
    chain_sent(0)
    places.wait_recv()

    attend(1)
    swap_context(1).start()
    reduce(1)
    residual.wait_recv()
    st[...] = rrb[...].astype(F32)
    rows = restore(1).astype(F32)
    for j in range(NSUB):
        v = rows[:, j * PART : (j + 1) * PART]
        pair = [swap(v[8 * h : 8 * h + 8, 0:TILE], v[8 * h : 8 * h + 8, TILE:PART]) for h in range(2)]
        for c in range(2):
            fsb[c, :, j * TILE : (j + 1) * TILE] = jnp.concatenate([pair[0][c], pair[1][c]], axis=0).astype(BF16)
    for c in range(2):
        final(c).start()

    residual.wait_send()
    a2a_all(1).wait_send()
    squares_all().wait_send()
    swap_context(1).wait_send()
    chain_sent(1)
    finals.wait_recv()
    got = [frb[c].astype(F32) for c in range(2)]
    pieces = []
    for jj in range(NZ):
        h, j = jj // 8, (jj % 8) // 2
        for c in range(2):
            v = got[c][8 * h : 8 * h + 8, j * TILE : (j + 1) * TILE]
            pieces.append(pltpu.roll(v, 4, 0) if jj % 2 else v)
    out[0] = jnp.concatenate(pieces, axis=1)[0:4].astype(BF16)
    finals.wait_send()


def per_device(hidden, norm_gain, q_gain, out_weight, positions):
    vmem = pl.BlockSpec(memory_space=pltpu.VMEM)
    dma = pltpu.SemaphoreType.DMA
    return pl.pallas_call(
        kernel,
        out_shape=jax.ShapeDtypeStruct(hidden.shape, BF16),
        in_specs=[pl.BlockSpec(memory_space=pltpu.HBM)] * 5,
        out_specs=vmem,
        scratch_shapes=[
            pltpu.VMEM((1, 4, 8192), BF16),
            pltpu.VMEM((1, 8192), F32),
            pltpu.VMEM((1, 8192), F32),
            pltpu.VMEM((1, TOK), jnp.int32),
            pltpu.VMEM((TILE, TILE), BF16),
            pltpu.VMEM((TILE, TILE), BF16),
            pltpu.VMEM((8, 8192), F32),
            pltpu.VMEM((16, HALF), F32),
            pltpu.VMEM((2, NZ, TILE, TILE), BF16),
            pltpu.VMEM((4, 16, 1024), BF16),
            pltpu.VMEM((2, 16, 1024), BF16),
            pltpu.VMEM((1, 8192), F32),
            pltpu.VMEM((1, TOK), jnp.int32),
            pltpu.VMEM((2, NZ, 16, HEAD), BF16),
            pltpu.VMEM((2, NZ, 16, HEAD), BF16),
            pltpu.VMEM((2, 2, TOK, TILE), BF16),
            pltpu.VMEM((NZ, 16, HALF), F32),
            pltpu.VMEM((2, 8, 2, 16, HALF), BF16),
            pltpu.VMEM((2, 8, 2, 16, HALF), BF16),
            pltpu.VMEM((2 * NZ, 1, TOK), F32),
            pltpu.VMEM((2 * NZ, 1, TOK), F32),
            pltpu.VMEM((16, HALF), BF16),
            pltpu.VMEM((16, HALF), BF16),
            pltpu.VMEM((2, 16, 1024), BF16),
            pltpu.VMEM((2, 16, 1024), BF16),
            pltpu.VMEM((7, 16, HEAD), BF16),
            dma((4,)),
            dma((4,)),
            dma((1,)),
            dma((4,)),
            dma((5,)),
            dma((5,)),
            dma((2,)),
            dma((2,)),
            dma((2,)),
            dma((2,)),
            dma((2, 2)),
            dma((2, 8, 2, 2)),
            dma((1,)),
            dma((1,)),
            dma((7,)),
            dma((7,)),
            dma((1,)),
            dma((1,)),
        ],
        compiler_params=pltpu.CompilerParams(
            collective_id=0, has_side_effects=True, vmem_limit_bytes=60 * 1024 * 1024
        ),
    )(hidden, norm_gain, q_gain, out_weight, positions)


def solution(mesh):
    return jax.shard_map(
        per_device,
        mesh=mesh,
        in_specs=(
            P("section", "tp", None),
            P("section", None),
            P("section", None),
            P("section", "tp", None),
            P("section", None),
        ),
        out_specs=P("section", "tp", None),
        check_vma=False,
    )
```
